32 devices in a mesh: rows: 16 (over z, y, x), cols: 2 (over core).
Axes of the slice: x: 2, y: 2, z: 4, core: 2. Of those that a mesh axis runs over, the one named last changes fastest.
Arguments:
- tokens: bfloat16 [16384, 768], P(('rows', 'cols')), may hold values from -6 to 6
- segment_ids: int32 [32, 512], P(('rows', 'cols')), may hold values from 0 to 3, as said below
- position_table: bfloat16 [512, 768], replicated, may hold values from -6 to 6
- table_gain: float32 [768], replicated, may hold values from 0.5 to 1.5
- table_shift: float32 [768], replicated, may hold values from -4 to 4
- query_weight: bfloat16 [768, 768], replicated, may hold values from -0.21875 to 0.21875
- key_weight: bfloat16 [768, 768], replicated, may hold values from -0.21875 to 0.21875
- value_weight: bfloat16 [768, 768], replicated, may hold values from -0.21875 to 0.21875
- output_weight: bfloat16 [768, 768], replicated, may hold values from -1.75 to 1.75
- first_gain: float32 [768], replicated, may hold values from 0.5 to 1.5
- first_shift: float32 [768], replicated, may hold values from -4 to 4
- feedforward_input_weight: bfloat16 [768, 3072], P(None, 'cols'), may hold values from -0.21875 to 0.21875
- ffn_out: bfloat16 [3072, 768], P('cols'), may hold values from -0.109375 to 0.109375
- second_gain: float32 [768], replicated, may hold values from 0.5 to 1.5
- second_shift: float32 [768], replicated, may hold values from -4 to 4
- out_grad: bfloat16 [16384, 768], P(('rows', 'cols')), may hold values from -6 to 6
Outputs:
- output: bfloat16 [16384, 768], P(('rows', 'cols'))
- tokens_grad: bfloat16 [16384, 768], P(('rows', 'cols'))
- position_table_grad: float32 [512, 768], replicated
- table_gain_grad: float32 [768], replicated
- table_shift_grad: float32 [768], replicated
- query_weight_grad: float32 [768, 768], replicated
- key_weight_grad: float32 [768, 768], replicated
- value_weight_grad: float32 [768, 768], replicated
- output_weight_grad: float32 [768, 768], replicated
- first_gain_grad: float32 [768], replicated
- first_shift_grad: float32 [768], replicated
- ffn_in_grad: float32 [768, 3072], P(None, 'cols')
- ffn_out_grad: float32 [3072, 768], P('cols')
- second_gain_grad: float32 [768], replicated
- second_shift_grad: float32 [768], replicated
The draws below stay inside these ranges and needn't reach their ends.
Inputs may be any that keep to these rules, and one draw needn't show every extreme that they name: `segment_ids`: within each packed row of 512 tokens the ids start at 0 and rise by one at the first token of each document, never falling; a row holds at most four documents.
All inputs are finite; a program needn't handle non-finite values.
Results may differ from the reference program's by a relative error of at most 0.017.
Values may be sent and summed in bfloat16 or wider, within the bound.
A program may use at most 256 MiB of HBM per device.

```python
import math
import jax
import jax.numpy as jnp
import numpy as np
from jax import lax

D = 768
HEADS = 12
HEAD_DIM = 64
FF = 3072
BUCKETS = 256
MAX_POS = 512
SEQ = 512
NROWS = 32
TOKENS = 16384


def draw_segment_ids(key, part):
    key = jax.random.fold_in(key, 11)
    key_place, key_count, key_forced = jax.random.split(key, 3)
    row_keys = jax.random.split(key_place, NROWS)
    begins = jax.vmap(lambda one: jax.random.permutation(one, SEQ - 1)[:3] + 1)(row_keys).astype(jnp.int32)
    counts = jax.random.randint(key_count, (NROWS,), 0, 4).astype(jnp.int32)
    forced = jax.random.randint(key_forced, (), 0, NROWS).astype(jnp.int32)
    counts = jnp.where(jnp.arange(NROWS, dtype=jnp.int32) == forced, 3, counts)
    active = jnp.arange(3, dtype=jnp.int32)[None, :] < counts[:, None]
    places = lax.broadcasted_iota(jnp.int32, (NROWS, SEQ), 1)
    hits = (places[:, :, None] == begins[:, None, :]) & active[:, None, :]
    starts = jnp.sum(hits.astype(jnp.int32), axis=2)
    return jnp.cumsum(starts, axis=1).astype(jnp.int32)


def shard_levels(key, dims, cuts, least, top_value):
    level, own = 1.0, jax.random.fold_in(key, 6)
    for dim, parts in cuts:
        steps = jnp.exp(jax.random.uniform(jax.random.fold_in(own, dim), (parts,), jnp.float32, least / len(cuts), top_value / len(cuts)))
        level = level * jnp.repeat(steps, dims[dim] // parts).reshape([-1 if axis == dim else 1 for axis in range(len(dims))])
    return level


def noise(own_key, extent, width, bound, cuts=(), kind=jnp.bfloat16):
    loudness = shard_levels(own_key, extent, cuts, -0.22, 0.18) if cuts else 1.0
    entries = jax.random.normal(own_key, extent, jnp.float32) * width * loudness
    return jnp.minimum(jnp.maximum(entries, -bound), bound).astype(kind)


def setup_inputs(seed: int = 0) -> dict:
    splits = jax.random.split(jax.random.key(seed), 17)
    return {
        "tokens": noise(splits[0], (TOKENS, D), 1.0, 6.0, ((0, 32),)),
        "segment_ids": draw_segment_ids(jax.random.fold_in(splits[16], 71), 0),
        "position_table": noise(splits[2], (2 * BUCKETS, D), 1.0, 6.0),
        "table_gain": jnp.clip(1.0 + 0.1 * jax.random.normal(splits[3], (D,), jnp.float32), 0.5, 1.5),
        "table_shift": noise(splits[4], (D,), 0.3, 4.0, (), jnp.float32),
        "query_weight": noise(splits[5], (D, D), D ** -0.5, 0.21875),
        "key_weight": noise(splits[6], (D, D), D ** -0.5, 0.21875),
        "value_weight": noise(splits[7], (D, D), D ** -0.5, 0.21875),
        "output_weight": noise(splits[8], (D, D), (D // 64) ** -0.5, 1.75),
        "first_gain": jnp.clip(1.0 + 0.1 * jax.random.normal(splits[9], (D,), jnp.float32), 0.5, 1.5),
        "first_shift": noise(splits[10], (D,), 0.3, 4.0, (), jnp.float32),
        "feedforward_input_weight": noise(splits[11], (D, FF), D ** -0.5, 0.21875, ((1, 2),)),
        "ffn_out": noise(splits[12], (FF, D), FF ** -0.5, 0.109375, ((0, 2),)),
        "second_gain": jnp.clip(1.0 + 0.1 * jax.random.normal(splits[13], (D,), jnp.float32), 0.5, 1.5),
        "second_shift": noise(splits[14], (D,), 0.3, 4.0, (), jnp.float32),
        "out_grad": noise(splits[15], (TOKENS, D), 1.0, 6.0, ((0, 32),)),
    }


EPSILON = 1e-07
NEGATIVE = -1e+30

@jax.custom_vjp
def low(v):
    return lax.optimization_barrier(v.astype(jnp.bfloat16)).astype(jnp.float32)

@jax.custom_vjp
def low_back(v):
    return v

def low_keep(v):
    return (low(v), None)

def low_pass(kept, grad):
    return (grad,)

def back_keep(v):
    return (v, None)

def back_low(kept, grad):
    return (low(grad),)
low.defvjp(low_keep, low_pass)
low_back.defvjp(back_keep, back_low)

def rounded(value):
    return low(low_back(value))

def matmul(left, right):
    return jnp.dot(left, right, precision=lax.Precision.HIGHEST)

def bucket_table(length):
    middle = BUCKETS // 2
    distance = np.arange(-(length - 1), length)
    direction = np.sign(distance)
    magnitude = np.where((distance < middle) & (distance > -middle), middle - 1, np.abs(distance))
    logged = np.ceil(np.log(magnitude / middle) / np.log((MAX_POS - 1) / middle) * (middle - 1)) + middle
    bucket = np.where(magnitude <= middle, distance, logged * direction)
    return np.clip(bucket + BUCKETS, 0, 2 * BUCKETS - 1).astype(np.int32)

def relative_index(segment_row):
    length = segment_row.shape[0]
    places = jnp.arange(length, dtype=jnp.int32)
    begins = jnp.concatenate([jnp.ones((1,), dtype=jnp.bool_), segment_row[1:] != segment_row[:-1]])
    starts = jnp.where(begins, places, jnp.zeros_like(places))
    positions = places - lax.cummax(starts, axis=0)
    offsets = positions[:, None] - positions[None, :] + (length - 1)
    index = jnp.take(jnp.asarray(bucket_table(length)), offsets).astype(jnp.int32)
    same = segment_row[:, None] == segment_row[None, :]
    return (index, same)

def normalize(value, gain, shift):
    centered = value - lax.optimization_barrier(jnp.mean(value, axis=-1, keepdims=True))
    squared_spread = lax.optimization_barrier(jnp.mean(centered * centered, axis=-1, keepdims=True))
    return centered * lax.rsqrt(squared_spread + EPSILON) * gain + shift

def attend_row(query_rows_all, key_matrix_rows, value_rows, segment_row, pos_keys, pos_queries):
    index, same = relative_index(segment_row)
    heads = query_rows_all.shape[1]
    highest = lax.Precision.HIGHEST
    content = jnp.einsum('ihd,jhd->hij', query_rows_all, key_matrix_rows, precision=highest)
    from_query = low_back(jnp.einsum('ihd,rhd->hir', query_rows_all, pos_keys, precision=highest))
    from_key = low_back(jnp.einsum('jhd,rhd->hjr', key_matrix_rows, pos_queries, precision=highest))
    wide = jnp.broadcast_to(index[None], (heads,) + index.shape)
    picked_query = jnp.take_along_axis(from_query, wide, axis=2)
    picked_key = jnp.swapaxes(jnp.take_along_axis(from_key, wide, axis=2), 1, 2)
    scores = low_back(content + picked_query + picked_key)
    masked = jnp.where(same[None], scores, NEGATIVE)
    top = lax.optimization_barrier(jnp.max(masked, axis=-1, keepdims=True))
    weights = jnp.where(same[None], jnp.exp(masked - top), 0.0)
    prob = weights / lax.optimization_barrier(jnp.sum(weights, axis=-1, keepdims=True))
    return jnp.einsum('hij,jhd->ihd', low(prob), value_rows, precision=highest)

def block_forward(token_block, segment_block, params):
    pos_keys, pos_queries, query_weight, key_weight, value_weight, output_weight, first_gain, first_shift, feedforward_input_weight, ffn_out, second_gain, second_shift = params
    factor = 1.0 / math.sqrt(3 * HEAD_DIM)
    count_rows = segment_block.shape[0]
    query_rows_all = rounded(matmul(token_block, query_weight) * factor)
    key_matrix_rows = rounded(matmul(token_block, key_weight))
    value_rows = rounded(matmul(token_block, value_weight))
    shaped = (query_rows_all.reshape(count_rows, SEQ, HEADS, HEAD_DIM), key_matrix_rows.reshape(count_rows, SEQ, HEADS, HEAD_DIM), value_rows.reshape(count_rows, SEQ, HEADS, HEAD_DIM), segment_block)

    def one_row(pieces):
        return attend_row(pieces[0], pieces[1], pieces[2], pieces[3], pos_keys, pos_queries)
    context = lax.map(jax.checkpoint(one_row), shaped)
    context = rounded(context.reshape(count_rows * SEQ, D))
    attn_out = low_back(matmul(context, output_weight))
    first = normalize(attn_out + token_block, first_gain, first_shift)
    inner = low_back(matmul(low(first), feedforward_input_weight))
    activation = low(jax.nn.gelu(inner, approximate=False))
    ffn_result = low_back(matmul(activation, ffn_out))
    return normalize(ffn_result + first, second_gain, second_shift)

def forward(tokens, position_table, table_gain, table_shift, query_weight, key_weight, value_weight, output_weight, first_gain, first_shift, feedforward_input_weight, ffn_out, second_gain, second_shift, segment_ids):
    factor = 1.0 / math.sqrt(3 * HEAD_DIM)
    pos_rows = low(normalize(position_table, table_gain, table_shift))
    pos_keys = rounded(matmul(pos_rows, key_weight)).reshape(2 * BUCKETS, HEADS, HEAD_DIM)
    pos_queries = rounded(matmul(pos_rows, query_weight) * factor).reshape(2 * BUCKETS, HEADS, HEAD_DIM)
    params = (pos_keys, pos_queries, query_weight, key_weight, value_weight, output_weight, first_gain, first_shift, feedforward_input_weight, ffn_out, second_gain, second_shift)
    group = math.gcd(NROWS, 8)
    blocks = NROWS // group
    token_blocks = tokens.reshape(blocks, group * SEQ, D)
    segment_blocks = segment_ids.reshape(blocks, group, SEQ)
    checked = jax.checkpoint(lambda token_block, segment_block: block_forward(token_block, segment_block, params))

    def step(carry, pieces):
        return (carry, checked(pieces[0], pieces[1]))
    carry_out, result = lax.scan(step, jnp.zeros((), jnp.float32), (token_blocks, segment_blocks))
    return result.reshape(TOKENS, D)

def reference(tokens, segment_ids, position_table, table_gain, table_shift, query_weight, key_weight, value_weight, output_weight, first_gain, first_shift, feedforward_input_weight, ffn_out, second_gain, second_shift, out_grad):
    float_values = tuple((item.astype(jnp.float32) for item in (tokens, position_table, table_gain, table_shift, query_weight, key_weight, value_weight, output_weight, first_gain, first_shift, feedforward_input_weight, ffn_out, second_gain, second_shift)))

    def wrapped(*values):
        return forward(*values, segment_ids)
    second, pullback = jax.vjp(wrapped, *float_values)
    grads = pullback(out_grad.astype(jnp.float32))
    return (second.astype(jnp.bfloat16), grads[0].astype(jnp.bfloat16), grads[1], grads[2], grads[3], grads[4], grads[5], grads[6], grads[7], grads[8], grads[9], grads[10], grads[11], grads[12], grads[13])
```

```python
import math

import jax
import jax.numpy as jnp
import numpy as np
from jax import lax
from jax.experimental import pallas as pl
from jax.experimental.pallas import tpu as pltpu
from jax.sharding import PartitionSpec as P

HEAD_DIM = 64
BUCKETS = 256
MAX_POS = 512
EPSILON = 1e-07
NEGATIVE = -1e30
ROOT_HALF = 0.7071067811865476
DENSITY_SCALE = 0.3989422804014327

LANES = 128
VMEM_BYTES = 56 * 1024 * 1024
GRADIENT_VMEM_BYTES = 60 * 1024 * 1024
F32 = jnp.float32
LOW = jnp.bfloat16


def bucket_table(length):
    middle = BUCKETS // 2
    distance = np.arange(-(length - 1), length)
    direction = np.sign(distance)
    magnitude = np.where((distance < middle) & (distance > -middle), middle - 1, np.abs(distance))
    logged = (
        np.ceil(np.log(magnitude / middle) / np.log((MAX_POS - 1) / middle) * (middle - 1)) + middle
    )
    bucket = np.where(magnitude <= middle, distance, logged * direction)
    return np.clip(bucket + BUCKETS, 0, 2 * BUCKETS - 1).astype(np.int32)


def spread_index(length):
    table = np.concatenate([bucket_table(length)[::-1], [-1]]).astype(np.int32)
    return table.reshape(1, 2 * length)


def dot(left, right):
    return jnp.dot(left, right, preferred_element_type=F32)


def dot_rows(left, right):
    return lax.dot_general(left, right, (((1,), (1,)), ((), ())), preferred_element_type=F32)


def dot_columns(left, right):
    return lax.dot_general(left, right, (((0,), (0,)), ((), ())), preferred_element_type=F32)


def norm_forward(value, gain, shift):
    centered = value - jnp.mean(value, axis=-1, keepdims=True)
    squared_spread = jnp.mean(centered * centered, axis=-1, keepdims=True)
    scale_rows = lax.rsqrt(squared_spread + EPSILON)
    normed = centered * scale_rows
    return (normed * gain + shift, normed, scale_rows)


def norm_backward(grad, normed, scale_rows, gain):
    scaled = grad * gain
    return scale_rows * (
        scaled
        - jnp.mean(scaled, axis=-1, keepdims=True)
        - normed * jnp.mean(scaled * normed, axis=-1, keepdims=True)
    )


def pair_columns(pair):
    return pl.ds(pl.multiple_of(pair * LANES, LANES), LANES)


def head_lanes(rows, half):
    lane = lax.broadcasted_iota(jnp.int32, (rows, LANES), 1)
    return (lane < HEAD_DIM) if half == 0 else (lane >= HEAD_DIM)


def spread_columns(index_ref, buckets):
    column = lax.broadcasted_iota(jnp.int32, (index_ref.shape[0], buckets), 1)
    return jnp.where(index_ref[...] == column, 1.0, 0.0).astype(LOW)


def spread_matrix(index_ref, buckets):
    row = lax.broadcasted_iota(jnp.int32, (buckets, index_ref.shape[1]), 0)
    return jnp.where(index_ref[...] == row, 1.0, 0.0).astype(LOW)


def flip_matrix():
    row = lax.broadcasted_iota(jnp.int32, (LANES, LANES), 0)
    column = lax.broadcasted_iota(jnp.int32, (LANES, LANES), 1)
    return jnp.where(row + column == LANES - 1, 1.0, 0.0).astype(LOW)


def unit_matrix():
    row = lax.broadcasted_iota(jnp.int32, (LANES, LANES), 0)
    column = lax.broadcasted_iota(jnp.int32, (LANES, LANES), 1)
    return jnp.where(row == column, 1.0, 0.0).astype(LOW)


def both_heads(pair_rows):
    rows = pair_rows.shape[0]
    return jnp.concatenate(
        [jnp.where(head_lanes(rows, half), pair_rows, 0) for half in range(2)], axis=0
    )


def join_heads(stacked):
    rows = stacked.shape[0] // 2
    return jnp.where(head_lanes(rows, 0), stacked[:rows], stacked[rows:])


def skewed(window, length):
    turned = pltpu.roll(window, length + 1, 1, stride=1, stride_axis=0)
    return turned[:, :length]


def unskewed(flipped):
    rows, length = flipped.shape
    wide = jnp.concatenate([flipped, jnp.zeros((rows, LANES), flipped.dtype)], axis=1)
    return pltpu.roll(wide, 0, 1, stride=1, stride_axis=0)


def as_row(vector):
    return vector[...].reshape(1, vector.shape[0])


def whole(shape):
    zeros = (0,) * len(shape)
    return pl.BlockSpec(shape, lambda *_: zeros, pipeline_mode=pl.Buffered(1))


def whole_out(shape):
    zeros = (0,) * len(shape)
    return pl.BlockSpec(shape, lambda *_: zeros)


def gelu_parts(value):
    size = jnp.abs(value) * ROOT_HALF
    part = 1.0 / (1.0 + 0.3275911 * size)
    bell = jnp.exp(-0.5 * value * value)
    series = 1.061405429 * part - 1.453152027
    series = series * part + 1.421413741
    series = series * part - 0.284496736
    series = series * part + 0.254829592
    tail = 0.5 * series * part * bell
    return jnp.where(value < 0.0, tail, 1.0 - tail), bell


class Mover:
    def __init__(self, sems):
        self.sems, self.count, self.open = sems, 0, []

    def start(self, source, target):
        copy = pltpu.make_async_copy(source, target, self.sems.at[self.count])
        self.count += 1
        copy.start()
        return copy

    def leave(self, source, target):
        self.open.append(self.start(source, target))

    def finish(self):
        for copy in self.open:
            copy.wait()


def unit_order(parts):
    return [(place % (parts // 2)) * 2 + place // (parts // 2) for place in range(parts)]


def forward_kernel(
    tokens,
    segments,
    table,
    table_gain,
    table_shift,
    query_weight,
    key_weight,
    value_weight,
    output_weight,
    first_gain,
    first_shift,
    in_weight,
    out_weight,
    second_gain,
    second_shift,
    out_grad,
    spread,
    query_out,
    key_out,
    value_out,
    prob_out,
    context_out,
    normed_out,
    scale_out,
    first_low_out,
    key_table_out,
    query_table_out,
    pos_rows_out,
    in_weights_out,
    out_weights_out,
    activation_out,
    slope_out,
    grad_pre2_out,
    output_out,
    vectors_out,
    rows_in,
    table_in,
    weights_in,
    out_grad_in,
    heads_in,
    tables_in,
    probs,
    context,
    normed,
    scale,
    first_low,
    total,
    in_weights,
    out_weights,
    inner,
    activation,
    slope,
    output,
    vectors,
    mask,
    crossed,
    send_sems,
    receive_sems,
    prob_sems,
    move_sems,
):
    length, width = tokens.shape
    parts, _, units = in_weights.shape
    factor = 1.0 / math.sqrt(3 * HEAD_DIM)
    row, me = lax.axis_index("rows"), lax.axis_index("cols")
    mover = Mover(move_sems)
    table_load = mover.start(table, table_in)
    key_load = mover.start(key_weight, weights_in.at[1])
    query_load = mover.start(query_weight, weights_in.at[0])
    tokens_load = mover.start(tokens, rows_in.at[pl.ds(0, length)])
    value_load = mover.start(value_weight, weights_in.at[2])
    output_load = mover.start(output_weight, weights_in.at[3])
    grad_load = mover.start(out_grad, out_grad_in)
    own_loads = [
        mover.start(in_weight, in_weights.at[me]),
        mover.start(out_weight, out_weights.at[me]),
    ]
    peers = [lax.rem(me + step, parts) for step in range(1, parts)]
    barrier = pltpu.get_barrier_semaphore()
    for peer in peers:
        pl.semaphore_signal(
            barrier, inc=1, device_id=(row, peer), device_id_type=pl.DeviceIdType.MESH
        )
    pl.semaphore_wait(barrier, parts - 1)

    def shard_copy(kind, step, place):
        source, target = ((in_weight, in_weights), (out_weight, out_weights))[kind]
        return pltpu.make_async_remote_copy(
            src_ref=source,
            dst_ref=target.at[place],
            send_sem=send_sems.at[kind, step],
            recv_sem=receive_sems.at[kind, step],
            device_id=(row, peers[step]),
            device_id_type=pl.DeviceIdType.MESH,
        )

    for kind in range(2):
        for step in range(parts - 1):
            shard_copy(kind, step, me).start()

    key_load.wait()
    query_load.wait()
    table_load.wait()
    pos_out, _, _ = norm_forward(table_in[...].astype(F32), as_row(table_gain), as_row(table_shift))
    pos_rows_in = rows_in.at[pl.ds(length, table.shape[0])]
    pos_rows_in[...] = pos_out.astype(LOW)
    mover.leave(pos_rows_in, pos_rows_out)
    matrix = spread_columns(spread, table.shape[0])
    tokens_load.wait()
    both = dot(rows_in[...], weights_in[1]).astype(LOW)
    heads_in[1] = both[:length]
    tables_in[0] = dot(matrix, both[length:]).astype(LOW)
    both = (dot(rows_in[...], weights_in[0]) * factor).astype(LOW)
    heads_in[0] = both[:length]
    tables_in[1] = dot(matrix, both[length:]).astype(LOW)
    mover.leave(tables_in.at[0], key_table_out)
    mover.leave(tables_in.at[1], query_table_out)
    value_load.wait()
    heads_in[2] = dot(rows_in[0:length, :], weights_in[2]).astype(LOW)
    for place, target in enumerate((query_out, key_out, value_out)):
        mover.leave(heads_in.at[place], target)
    document = lax.broadcasted_iota(jnp.int32, (8, length), 0)
    member = jnp.where(segments[...] == document, 1.0, 0.0).astype(LOW)
    mask[...] = jnp.where(dot_columns(member, member) > 0.5, 0.0, NEGATIVE)

    blocks = [slice(at * LANES, (at + 1) * LANES) for at in range(length // LANES)]
    unit = unit_matrix()

    pairs = width // LANES

    def prob_copy(pair):
        heads = pl.ds(2 * pair, 2)
        return pltpu.make_async_copy(probs.at[heads], prob_out.at[heads], prob_sems.at[pair])

    def cross(pair, rows, side):
        columns = pair_columns(pair)
        start = length - rows.stop
        keys = both_heads(heads_in[1, rows, columns])
        window = dot_rows(keys, tables_in[1, start : start + length + LANES, columns])
        for half in range(2):
            part = window[half * LANES : (half + 1) * LANES]
            crossed[side, half, rows, :] = skewed(part, length).astype(LOW)

    def weigh(pair, rows, side):
        columns = pair_columns(pair)
        start = length - rows.stop
        queries = both_heads(heads_in[0, rows, columns])
        key_pair = heads_in[1, :, columns]
        window = dot_rows(queries, tables_in[0, start : start + length + LANES, columns])
        for half in range(2):
            span = slice(half * LANES, (half + 1) * LANES)
            left = jnp.concatenate([queries[span], unit], axis=1)
            right = jnp.concatenate([key_pair, crossed[side, half, :, rows]], axis=1)
            scores = dot_rows(left, right) + skewed(window[span], length) + mask[rows, :]
            top = jnp.max(scores, axis=-1, keepdims=True)
            weights = jnp.exp(scores - top)
            share = jnp.sum(weights, axis=-1, keepdims=True)
            probs[2 * pair + half, rows, :] = (weights * (1.0 / share)).astype(LOW)

    def two_pairs(step, carry):
        for side in range(2):
            pair = 2 * step + side
            following = lax.min(pair + 1, pairs - 1)
            columns = pair_columns(pair)
            for rows in blocks:
                cross(following, rows, 1 - side)
                weigh(pair, rows, side)
            value_pair = heads_in[2, :, columns]
            contexts = [dot(probs[2 * pair + half], value_pair) for half in range(2)]
            joined = jnp.where(head_lanes(length, 0), contexts[0], contexts[1])
            context[:, columns] = joined.astype(LOW)
            prob_copy(pair).start()
        return carry

    for rows in blocks:
        cross(0, rows, 0)
    lax.fori_loop(0, pairs // 2, two_pairs, 0)
    mover.leave(context, context_out)

    output_load.wait()
    halves = [slice(at, at + length // 2) for at in range(0, length, length // 2)]
    for rows in halves:
        pre = dot(context[rows, :], weights_in[3]) + rows_in[rows, :].astype(F32)
        first, first_normed, scale_rows = norm_forward(pre, as_row(first_gain), as_row(first_shift))
        total[rows, :] = first
        first_low[rows, :] = first.astype(LOW)
        normed[rows, :] = first_normed
        scale[rows, :] = scale_rows
    mover.leave(first_low, first_low_out)
    mover.leave(normed, normed_out)
    mover.leave(scale, scale_out)

    for copy in own_loads:
        copy.wait()
    for kind in range(2):
        for step in range(parts - 1):
            shard_copy(kind, step, lax.rem(me + parts - 1 - step, parts)).wait_recv()
    mover.leave(in_weights, in_weights_out)
    mover.leave(out_weights, out_weights_out)
    size = math.gcd(units, width)
    chunks = [
        (part, slice(at, at + size)) for part in unit_order(parts) for at in range(0, units, size)
    ]

    def begin(number):
        part, cut = chunks[number]
        inner[number % 2] = dot(first_low[...], in_weights[part, :, cut])

    begin(0)
    for number, (part, cut) in enumerate(chunks):
        columns = slice(number * size, (number + 1) * size)
        if number + 1 < len(chunks):
            begin(number + 1)
        for rows in halves:
            value = inner[number % 2, rows, :]
            cumulative, bell = gelu_parts(value)
            activation[rows, columns] = (value * cumulative).astype(LOW)
            slope[rows, columns] = (cumulative + value * bell * DENSITY_SCALE).astype(LOW)
        total[...] += dot(activation[:, columns], out_weights[part, cut, :])
        mover.leave(activation.at[:, columns], activation_out.at[:, columns])
        mover.leave(slope.at[:, columns], slope_out.at[:, columns])
    grad_load.wait()
    gain_sum = jnp.zeros((1, width), F32)
    shift_sum = jnp.zeros((1, width), F32)
    for rows in halves:
        second, second_normed, scale_rows = norm_forward(
            total[rows, :], as_row(second_gain), as_row(second_shift)
        )
        output[rows, :] = second.astype(LOW)
        grad_out = out_grad_in[rows, :].astype(F32)
        gain_sum = gain_sum + jnp.sum(grad_out * second_normed, axis=0, keepdims=True)
        shift_sum = shift_sum + jnp.sum(grad_out, axis=0, keepdims=True)
        total[rows, :] = norm_backward(grad_out, second_normed, scale_rows, as_row(second_gain))
    mover.leave(total, grad_pre2_out)
    mover.leave(output, output_out)
    vectors[0:1, :] = gain_sum
    vectors[1:2, :] = shift_sum
    vectors[2:8, :] = jnp.zeros((6, width), F32)
    mover.leave(vectors, vectors_out)
    for kind in range(2):
        for step in range(parts - 1):
            shard_copy(kind, step, me).wait_send()
    for pair in range(pairs):
        prob_copy(pair).wait()
    mover.finish()


def forward(
    tokens,
    segment_ids,
    table,
    table_gain,
    table_shift,
    query_weight,
    key_weight,
    value_weight,
    output_weight,
    first_gain,
    first_shift,
    in_weight,
    out_weight,
    second_gain,
    second_shift,
    out_grad,
):
    length, width = tokens.shape
    heads = width // HEAD_DIM
    parts, units = lax.axis_size("cols"), in_weight.shape[1]
    hidden = parts * units
    chunk = math.gcd(units, width)
    inputs = (
        tokens,
        segment_ids,
        table,
        table_gain,
        table_shift,
        query_weight,
        key_weight,
        value_weight,
        output_weight,
        first_gain,
        first_shift,
        in_weight,
        out_weight,
        second_gain,
        second_shift,
        out_grad,
        jnp.asarray(spread_index(length).reshape(2 * length, 1)),
    )
    anywhere = pl.BlockSpec(memory_space=pl.ANY)
    local = pl.BlockSpec(memory_space=pltpu.VMEM)
    in_specs = [local if at in (1, 3, 4, 9, 10, 13, 14, 16) else anywhere for at in range(17)]

    def low(*shape):
        return jax.ShapeDtypeStruct(shape, LOW)

    def wide(*shape):
        return jax.ShapeDtypeStruct(shape, F32)

    outs = [
        low(length, width),
        low(length, width),
        low(length, width),
        low(heads, length, length),
        low(length, width),
        wide(length, width),
        wide(length, 1),
        low(length, width),
        low(2 * length, width),
        low(2 * length, width),
        low(*table.shape),
        low(parts, width, units),
        low(parts, units, width),
        low(length, hidden),
        low(length, hidden),
        wide(length, width),
        low(length, width),
        wide(8, width),
    ]
    scratch = [
        pltpu.VMEM((length + table.shape[0], width), LOW),
        pltpu.VMEM(table.shape, LOW),
        pltpu.VMEM((4, width, width), LOW),
        pltpu.VMEM((length, width), LOW),
        pltpu.VMEM((3, length, width), LOW),
        pltpu.VMEM((2, 2 * length, width), LOW),
        pltpu.VMEM((heads, length, length), LOW),
        pltpu.VMEM((length, width), LOW),
        pltpu.VMEM((length, width), F32),
        pltpu.VMEM((length, 1), F32),
        pltpu.VMEM((length, width), LOW),
        pltpu.VMEM((length, width), F32),
        pltpu.VMEM((parts, width, units), LOW),
        pltpu.VMEM((parts, units, width), LOW),
        pltpu.VMEM((2, length, chunk), F32),
        pltpu.VMEM((length, hidden), LOW),
        pltpu.VMEM((length, hidden), LOW),
        pltpu.VMEM((length, width), LOW),
        pltpu.VMEM((8, width), F32),
        pltpu.VMEM((length, length), F32),
        pltpu.VMEM((2, 2, length, length), LOW),
        pltpu.SemaphoreType.DMA((2, parts - 1)),
        pltpu.SemaphoreType.DMA((2, parts - 1)),
        pltpu.SemaphoreType.DMA((heads // 2,)),
        pltpu.SemaphoreType.DMA((24 + 2 * (hidden // chunk),)),
    ]
    return pl.pallas_call(
        forward_kernel,
        in_specs=in_specs,
        out_specs=[anywhere] * len(outs),
        out_shape=outs,
        scratch_shapes=scratch,
        compiler_params=pltpu.CompilerParams(
            vmem_limit_bytes=VMEM_BYTES, collective_id=1, has_side_effects=True
        ),
        name="forward",
    )(*inputs)


def split_flip(matrix, value):
    high = value.astype(LOW)
    rest = (value - high.astype(F32)).astype(LOW)
    return dot(matrix, high) + dot(matrix, rest)


PAIR_BITS = 4
TABLE_JOBS = 12
JOB_COUNT = 14
LEAVING = 3
THIRDS = 3
ORDERS = (
    (0, 2, 1, 3),
    (1, 2, 0, 3),
    (0, 1, 2, 3),
    (1, 0, 2, 3),
    (2, 0, 1, 3),
    (2, 1, 0, 3),
    (0, 2, 3, 1),
    (1, 2, 3, 0),
)
COLOURS = (5, 1, 2, 2, 1, 4, 4, 3, 0, 1, 2, 3, 4, 2)
TASKS_AFTER = {
    ("out", 1): (
        (0, 0), (1, 0),
    ),
    ("in", 0): (
        (2, 0),
    ),
    ("in", 1): (
        (4, 0), (3, 0), (5, 0),
    ),
    ("norm", 0): (
        (0, 1), (1, 1), (14, 0),
    ),
    ("context", 0): (
        (7, 0), (14, 1),
    ),
    ("prepare", 0): (
        (5, 1), (14, 2),
    ),
    ("head", 0): (
        (4, 1), (6, 0),
    ),
    ("head", 1): (
        (8, 0),
    ),
    ("head", 2): (
        (14, 3),
    ),
    ("head", 4): (
        (3, 1), (5, 2), (14, 4),
    ),
    ("head", 6): (
        (4, 2), (14, 5),
    ),
    ("head", 8): (
        (1, 2), (0, 2), (2, 1), (8, 1), (7, 1),
    ),
    ("head", 9): (
        (4, 3), (5, 3), (9, 0), (3, 2),
    ),
    ("head", 12): (
        (4, 4), (2, 2),
    ),
    ("head", 13): (
        (0, 3), (7, 2), (10, 0),
    ),
    ("head", 15): (
        (1, 3), (4, 5),
    ),
    ("head", 16): (
        (9, 1), (8, 2), (3, 3),
    ),
    ("head", 17): (
        (6, 1), (7, 3),
    ),
    ("table", 0): (
        (8, 3), (11, 0), (12, 0), (3, 4), (4, 6), (0, 4), (6, 2), (7, 4), (13, 0), (8, 4),
        (3, 5), (9, 2), (5, 4), (0, 5), (10, 1), (6, 3), (8, 5), (1, 4), (12, 1), (7, 5),
        (5, 5), (11, 1), (9, 3), (12, 2), (3, 6), (6, 4), (13, 1), (10, 2), (5, 6), (9, 4),
        (7, 6), (4, 7), (11, 2), (12, 3), (10, 3), (9, 5), (8, 6), (11, 3), (6, 5), (1, 5),
        (0, 6), (3, 7), (10, 4), (11, 4), (13, 2), (10, 5), (9, 6), (12, 4), (13, 3),
        (7, 7), (2, 3),
    ),
    ("tail", 0): (
        (12, 5), (8, 7), (11, 5), (2, 4), (1, 6), (13, 4), (10, 6), (9, 7), (0, 7), (6, 6),
        (11, 6), (12, 6), (2, 5), (13, 5), (13, 6), (8, 8), (12, 7), (2, 6), (10, 7),
        (11, 7), (13, 7), (6, 7), (2, 7), (9, 8), (7, 8), (12, 8), (8, 9), (1, 7), (5, 7),
        (3, 8), (10, 8), (13, 8), (9, 9), (4, 8), (12, 9), (13, 9), (0, 8), (11, 8), (6, 8),
        (11, 9), (2, 8), (10, 9), (5, 8), (1, 8),
    ),
}


class Job:
    def __init__(self, number, rows, colour, slot, lift, gathered):
        self.number, self.rows, self.colour = number, rows, colour
        self.slot, self.lift, self.gathered = slot, lift, gathered

    def received(self, stage):
        start = sum(self.rows >> (step + 1) for step in range(stage))
        return (self.lift // 16 * 15) + start, self.rows >> (stage + 1)


def make_jobs(height, table):
    jobs = [Job(n, height, COLOURS[n], n, 0, n >= 8) for n in range(TABLE_JOBS)]
    jobs.append(Job(TABLE_JOBS, table // 2, COLOURS[TABLE_JOBS], TABLE_JOBS, 0, True))
    jobs.append(Job(TABLE_JOBS + 1, table // 2, COLOURS[TABLE_JOBS + 1], TABLE_JOBS, table // 2, True))
    return jobs


class Exchange:
    def __init__(self, partial, landed, received, send_sems, receive_sems, outs, jobs):
        self.partial, self.landed, self.received = partial, landed, received
        self.send_sems, self.receive_sems = send_sems, receive_sems
        self.outs, self.jobs = outs, jobs
        row, column = lax.axis_index("rows"), lax.axis_index("cols")
        self.core = column % 2
        self.twin = (row, column + 1 - 2 * self.core)
        self.bits = [(row // (1 << bit)) % 2 for bit in range(PAIR_BITS)]
        self.partners = [
            (row + (1 - 2 * self.bits[bit]) * (1 << bit), column) for bit in range(PAIR_BITS)
        ]
        self.spans = {}
        for rows, colour in sorted({(job.rows, job.colour) for job in jobs}):
            base, size, kept, sent = 0, rows, [], []
            for bit in ORDERS[colour]:
                size //= 2
                sent.append((base + (1 - self.bits[bit]) * size, size))
                base = base + self.bits[bit] * size
                kept.append((base, size))
            self.spans[rows, colour] = (kept, sent)

    def greet(self):
        barrier = pltpu.get_barrier_semaphore()
        for partner in [self.twin] + self.partners:
            pl.semaphore_signal(
                barrier, inc=1, device_id=partner, device_id_type=pl.DeviceIdType.MESH
            )
        pl.semaphore_wait(barrier, 1 + PAIR_BITS)

    def copy(self, job, stage, source, target, partner):
        return pltpu.make_async_remote_copy(
            src_ref=source,
            dst_ref=target,
            send_sem=self.send_sems.at[job.number, stage],
            recv_sem=self.receive_sems.at[job.number, stage],
            device_id=partner,
            device_id_type=pl.DeviceIdType.MESH,
        )

    def rows_of(self, job, span):
        start, size = span
        return pl.ds(pl.multiple_of(job.lift + start, 16), size)

    def stage(self, job, stage):
        kept, sent = self.spans[job.rows, job.colour]
        order = ORDERS[job.colour]
        if stage < 4:
            source = self.partial.at[job.slot, self.rows_of(job, sent[stage])]
            start, size = job.received(stage)
            target = self.received.at[job.slot, pl.ds(start, size)]
            return self.copy(job, stage, source, target, self.partners[order[stage]])
        if stage < 8:
            source = self.landed.at[job.slot, self.rows_of(job, kept[7 - stage])]
            return self.copy(job, stage, source, source, self.partners[order[7 - stage]])
        rows = pl.ds(job.lift, job.rows)
        return self.copy(
            job, stage, self.landed.at[job.slot, rows], self.outs[job.number], self.twin
        )

    def arrival(self, job, stage):
        kept, sent = self.spans[job.rows, job.colour]
        if 4 <= stage < 8:
            target = self.landed.at[job.slot, self.rows_of(job, sent[7 - stage])]
            order = ORDERS[job.colour]
            return self.copy(job, stage, target, target, self.partners[order[7 - stage]])
        return self.stage(job, stage)

    def twin_copy(self, job, source):
        target = self.landed.at[job.slot, pl.ds(job.lift, job.rows)]
        return self.copy(job, 9, source, target, self.twin)

    def keep_copy(self, job):
        return pltpu.make_async_copy(
            self.landed.at[job.slot, pl.ds(job.lift, job.rows)],
            self.outs[job.number],
            self.send_sems.at[job.number, 10],
        )

    def run(self, number, task):
        job = self.jobs[number]
        kept, _ = self.spans[job.rows, job.colour]
        if task == 0:
            rows = pl.ds(job.lift, job.rows)
            self.twin_copy(job, self.landed.at[job.slot, rows]).wait_recv()
            self.partial[job.slot, rows, :] += self.landed[job.slot, rows, :]
        elif task <= 4:
            self.arrival(job, task - 1).wait_recv()
            start, size = job.received(task - 1)
            rows = self.rows_of(job, kept[task - 1])
            total = self.partial[job.slot, rows, :] + self.received[job.slot, pl.ds(start, size), :]
            if task < 4:
                self.partial[job.slot, rows, :] = total
            else:
                self.landed[job.slot, rows, :] = total
        elif task <= 8:
            self.arrival(job, task - 1).wait_recv()
        if task < 8:
            self.stage(job, task).start()
        elif task == 8:
            self.keep_copy(job).start()
            if job.gathered:
                self.stage(job, 8).start()
        else:
            self.arrival(job, 8).wait_recv()

    def finish(self):
        for job in self.jobs:
            for stage in range(8):
                self.stage(job, stage).wait_send()
            if job.gathered:
                self.stage(job, 8).wait_send()
            self.keep_copy(job).wait()


def gradient_kernel(
    activation,
    slope,
    in_weights,
    out_weights,
    first_low,
    grad_pre2,
    normed1,
    scale1,
    first_gain,
    output_weight,
    vectors,
    context,
    prob,
    query,
    key,
    value,
    key_table,
    query_table,
    tokens,
    pos_rows,
    query_weight,
    key_weight,
    value_weight,
    spread,
    in_share,
    out_share,
    heads_share,
    output_share,
    table_share,
    tokens_grad,
    vector_sums,
    partial,
    landed,
    received,
    leaving,
    hidden,
    narrow,
    heads_in,
    tables_in,
    weights_in,
    turned,
    grad_scores,
    flip_sums,
    key_turned_sum,
    query_turned_sum,
    value_turned_sum,
    table_sum,
    matrix,
    grad_pos_keys,
    grad_pos_queries,
    grad_total,
    normed_in,
    scale_in,
    vector_steps,
    vector_received,
    send_sems,
    receive_sems,
    vector_send_sems,
    vector_receive_sems,
    prob_sems,
    load_sems,
):
    length, width = tokens.shape
    parts, _, units = in_weights.shape
    table = pos_rows.shape[0]
    half = width // 2
    factor = 1.0 / math.sqrt(3 * HEAD_DIM)
    core = lax.axis_index("cols") % 2
    own = pl.multiple_of(core * half, half)
    jobs = make_jobs(width, table)
    outs = []
    for chunk in range(2):
        for part in range(2):
            outs.append(out_share.at[pl.ds(chunk * width, width), pl.ds(part * half, half)])
    for chunk in range(2):
        for part in range(2):
            outs.append(in_share.at[:, pl.ds(chunk * width + part * half, half)])
    outs.append(output_share.at[:, pl.ds(own, half)])
    for third in range(THIRDS):
        outs.append(heads_share.at[2 * third + core])
    for part in range(2):
        outs.append(table_share.at[pl.ds(part * table // 2, table // 2), pl.ds(own, half)])
    exchange = Exchange(partial, landed, received, send_sems, receive_sems, outs, jobs)
    mover = Mover(load_sems)

    sides = ((1 - core, 0), (core, 0), (1 - core, 1), (core, 1))

    def hidden_columns(number):
        side, chunk = sides[number]
        return pl.ds(pl.multiple_of(side * 2 * width + chunk * width, width), width)

    def load_weights(number):
        side, chunk = sides[number]
        piece = min(units, width)
        copies = []
        for start in range(0, width, piece):
            unit = chunk * width + start
            part, offset = 2 * (unit // units) + side, unit % units
            inside = pl.ds(start, piece)
            copies.append(
                mover.start(
                    out_weights.at[part, pl.ds(offset, piece)],
                    weights_in.at[2 + number % 2, inside],
                )
            )
            copies.append(
                mover.start(
                    in_weights.at[part, :, pl.ds(offset, piece)],
                    weights_in.at[number % 2, :, inside],
                )
            )
        return copies

    def load_hidden(source, number, slot):
        return mover.start(source.at[:, hidden_columns(number)], hidden.at[slot // 2, slot % 2])

    total_load = mover.start(grad_pre2, grad_total)
    active_loads = [load_hidden(activation, number, number) for number in range(4)]
    first_load = mover.start(first_low, narrow.at[0])
    weight_loads = [load_weights(number) for number in range(2)]
    vector_load = mover.start(vectors, vector_steps.at[0])
    norm_loads = (mover.start(normed1, normed_in), mover.start(scale1, scale_in))
    context_load = mover.start(context, narrow.at[2])
    head_loads = [
        mover.start(item, heads_in.at[place]) for place, item in enumerate((query, key, value))
    ]
    head_loads += [
        mover.start(key_table, tables_in.at[0]),
        mover.start(query_table, tables_in.at[1]),
    ]
    exchange.greet()

    def run_tasks(name):
        for number, task in TASKS_AFTER.get(name, ()):
            if number < JOB_COUNT:
                exchange.run(number, task)
            else:
                vector_task(task)

    vector_partners = [exchange.twin] + exchange.partners

    def vector_copy(step):
        return pltpu.make_async_remote_copy(
            src_ref=vector_steps.at[step],
            dst_ref=vector_received.at[step],
            send_sem=vector_send_sems.at[step],
            recv_sem=vector_receive_sems.at[step],
            device_id=vector_partners[step],
            device_id_type=pl.DeviceIdType.MESH,
        )

    def vector_task(step):
        if step > 0:
            vector_copy(step - 1).wait_recv()
            vector_steps[step] = vector_steps[step - 1] + vector_received[step - 1]
        if step < len(vector_partners):
            vector_copy(step).start()
        else:
            vector_sums[...] = vector_steps[step]

    def leaving_copy(number):
        job = jobs[number]
        return exchange.twin_copy(job, leaving.at[number % LEAVING, pl.ds(0, job.rows)])

    def open_space(number):
        if number >= LEAVING:
            leaving_copy(number - LEAVING).wait_send()
        return leaving.at[number % LEAVING, pl.ds(0, jobs[number].rows)]

    lower = [slice(0, half), slice(half, width)]

    def place_hidden(side, number, part_of):
        if side == 0:
            targets = [open_space(number), open_space(number + 1)]
        else:
            targets = [partial.at[number], partial.at[number + 1]]
        for rows in lower:
            value = part_of(rows).astype(LOW)
            for target, columns in zip(targets, lower):
                target[rows, :] = value[:, columns]
        if side == 0:
            leaving_copy(number).start()
            leaving_copy(number + 1).start()

    def place_halves(number, rows_list, part_of):
        job = jobs[number]
        space = open_space(number)
        for rows in rows_list:
            value = part_of(rows).astype(LOW)
            left, right = value[:, :half], value[:, half:]
            inside = pl.ds(job.lift + rows.start, rows.stop - rows.start)
            space[rows, :] = jnp.where(core == 0, right, left)
            partial[job.slot, inside, :] = jnp.where(core == 0, left, right)
        leaving_copy(number).start()

    total_load.wait()
    grad_ffn = narrow.at[1]
    grad_ffn[...] = grad_total[...].astype(LOW)
    slope_loads = []
    for number in range(4):
        side, chunk = number % 2, number // 2
        active_loads[number].wait()
        space = hidden.at[number // 2, number % 2]
        place_hidden(side, 2 * chunk, lambda rows: dot_columns(space[:, rows], grad_ffn[...]))
        slope_loads.append(load_hidden(slope, number, number))
        if side == 1:
            run_tasks(("out", chunk))

    first_load.wait()
    first_turned = turned.at[0]
    first_turned[...] = narrow[0].T
    token_loads = [mover.start(tokens, narrow.at[0])]
    for number in range(4):
        side, chunk = number % 2, number // 2
        for copy in weight_loads[number]:
            copy.wait()
        slope_loads[number].wait()
        space = hidden.at[number // 2, number % 2]
        part = dot_rows(grad_ffn[...], weights_in[2 + number % 2])
        space[...] = (part * space[...].astype(F32)).astype(LOW)
        place_hidden(side, 4 + 2 * chunk, lambda rows: dot(first_turned[rows, :], space[...]))
        grad_total[...] += dot_rows(space[...], weights_in[number % 2])
        if number + 2 < 4:
            weight_loads.append(load_weights(number + 2))
        run_tasks(("in", number))

    token_loads.append(mover.start(pos_rows, narrow.at[1]))
    output_load = mover.start(output_weight, weights_in.at[0])
    late_loads = [
        mover.start(item, weights_in.at[1 + place])
        for place, item in enumerate((query_weight, key_weight, value_weight))
    ]

    def prob_load(pair, slot):
        return pltpu.make_async_copy(
            prob.at[pl.ds(2 * pair, 2)],
            hidden.at[slot, :, :, pl.ds(0, length)],
            prob_sems.at[slot],
        )

    prob_load(0, 0).start()

    for copy in norm_loads:
        copy.wait()
    vector_load.wait()
    grad_first = grad_total[...]
    vector_steps[0, 2:3, :] = jnp.sum(grad_first * normed_in[...], axis=0, keepdims=True)
    vector_steps[0, 3:4, :] = jnp.sum(grad_first, axis=0, keepdims=True)
    grad_total[...] = norm_backward(grad_first, normed_in[...], scale_in[...], as_row(first_gain))
    narrow[3] = grad_total[...].astype(LOW)
    output_load.wait()
    heads_in[3] = dot_rows(narrow[3], weights_in[0]).astype(LOW)
    run_tasks(("norm", 0))

    context_load.wait()
    context_turned = turned.at[1]
    context_turned[...] = narrow[2].T

    place_halves(8, lower, lambda rows: dot(context_turned[rows, :], narrow[3]))
    run_tasks(("context", 0))

    for copy in head_loads:
        copy.wait()
    flip = flip_matrix()
    matrix[...] = spread_matrix(spread, table)
    (
        query_turned,
        grad_turned,
        query_flip_turned,
        key_flip_turned,
        key_turned,
        tokens_turned,
        pos_turned,
    ) = (turned.at[place] for place in range(7))
    for copy in token_loads:
        copy.wait()
    tokens_turned[...] = narrow[0].T
    pos_turned[...] = narrow[1].T
    grads = narrow
    query_in, key_in, value_in, grad_in = (heads_in.at[place] for place in range(4))
    query_turned[...] = query_in[...].T
    key_turned[...] = key_in[...].T
    grad_turned[...] = grad_in[...].T
    blocks = [slice(at * LANES, (at + 1) * LANES) for at in range(length // LANES)]
    for rows in blocks:
        query_flip_turned[:, rows] = dot(flip, query_in[rows, :]).astype(LOW).T
        key_flip_turned[:, rows] = dot(flip, key_in[rows, :]).astype(LOW).T
    run_tasks(("prepare", 0))

    spans = [slice(side * HEAD_DIM, (side + 1) * HEAD_DIM) for side in range(2)]

    def unskew_pair(pair, straight_turned, flip_turned, table_in, scores_of, turned_sum, table_sum):
        columns = pair_columns(pair)
        head_rows = [
            pl.ds(pl.multiple_of(pair * LANES + side * HEAD_DIM, HEAD_DIM), HEAD_DIM)
            for side in range(2)
        ]
        table_sum[...] = jnp.zeros_like(table_sum)
        straight = [None, None]
        flips = []
        for rows in blocks:
            start = length - rows.stop
            window = slice(start, start + length + LANES)
            moved = []
            for side in range(2):
                left = jnp.concatenate([flip, straight_turned[head_rows[side], rows]], axis=0)
                mixed = scores_of(left, side, rows)
                part = mixed[LANES:]
                straight[side] = part if straight[side] is None else straight[side] + part
                moved.append(unskewed(mixed[:LANES]).astype(LOW))
            for side in range(2):
                table_sum[spans[side], window] += dot(
                    flip_turned[head_rows[side], rows], moved[side]
                )
            stacked = dot(jnp.concatenate(moved, axis=0), table_in[window, columns])
            flips.append(join_heads(stacked))
        for side in range(2):
            turned_sum[spans[side], :] = straight[side]
        return flips

    def pair_tasks(pair, phase):
        for place in range(width // LANES):
            name = ("head", 3 * place + phase)
            if name in TASKS_AFTER:

                @pl.when(pair == place)
                def _():
                    run_tasks(name)

    def send_third(third):
        number = TABLE_JOBS - THIRDS + third
        wide = 2 * LANES
        columns = pl.ds(pl.multiple_of(third * wide, wide), wide)
        job = Job(number, width, 0, number, 0, True)
        before = Job(number - LEAVING, width, 0, number - LEAVING, 0, True)
        space = leaving.at[lax.rem(number, LEAVING)]
        exchange.twin_copy(before, space).wait_send()
        query_grad = dot(tokens_turned[...], grads[0, :, columns])
        query_grad = query_grad + dot_rows(pos_turned[...], grad_pos_queries[columns, :])
        key_grad = dot(tokens_turned[...], grads[1, :, columns])
        key_grad = key_grad + dot_rows(pos_turned[...], grad_pos_keys[columns, :])
        value_grad = dot(tokens_turned[...], grads[2, :, columns])
        for place, value in enumerate((query_grad * factor, key_grad, value_grad)):
            lanes = slice(place * LANES, (place + 1) * LANES)
            low, high = value[:, :LANES].astype(LOW), value[:, LANES:].astype(LOW)
            space[:, lanes] = jnp.where(core == 0, high, low)
            partial[number, :, lanes] = jnp.where(core == 0, low, high)
        exchange.twin_copy(job, space).start()

    def pair_back(pair, carry):
        slot = lax.rem(pair, 2)
        columns = pair_columns(pair)
        pair_rows = pl.ds(pl.multiple_of(pair * LANES, LANES), LANES)
        prob_load(pair, slot).wait()

        @pl.when(pair + 1 < width // LANES)
        def _():
            prob_load(pair + 1, 1 - slot).start()

        value_pair = value_in[:, columns]
        for rows in blocks:
            grad_probs = dot_rows(both_heads(grad_in[rows, columns]), value_pair)
            for side in range(2):
                weights = hidden[slot, side, rows, 0:length].astype(F32)
                product = grad_probs[side * LANES : (side + 1) * LANES] * weights
                shared = jnp.sum(product, axis=-1, keepdims=True)
                grad_scores[side, rows, :] = (product - weights * shared).astype(LOW)
        for side in range(2):
            head_rows = pl.ds(
                pl.multiple_of(pair * LANES + side * HEAD_DIM, HEAD_DIM), HEAD_DIM
            )
            value_turned_sum[spans[side], :] = dot(
                grad_turned[head_rows, :], hidden[slot, side, :, 0:length]
            )
        grads[2, :, columns] = value_turned_sum[...].astype(LOW).T
        pair_tasks(pair, 0)
        flips = unskew_pair(
            pair,
            query_turned,
            query_flip_turned,
            tables_in.at[0],
            lambda left, side, rows: dot(left, grad_scores[side, rows, :]),
            key_turned_sum,
            table_sum,
        )
        for rows, part in zip(blocks, flips):
            flip_sums[rows, :] = split_flip(flip, part)
        summed = dot_rows(table_sum[...].astype(LOW), matrix[...])
        grad_pos_keys[pair_rows, :] = summed.astype(LOW)
        pair_tasks(pair, 1)
        flips = unskew_pair(
            pair,
            key_turned,
            key_flip_turned,
            tables_in.at[1],
            lambda left, side, rows: dot_rows(left, grad_scores[side, :, rows]),
            query_turned_sum,
            table_sum,
        )
        for rows, part in zip(blocks, flips):
            summed = key_turned_sum[:, rows].T + split_flip(flip, part)
            grads[1, rows, columns] = summed.astype(LOW)
            summed = query_turned_sum[:, rows].T + flip_sums[rows, :]
            grads[0, rows, columns] = summed.astype(LOW)
        summed = dot_rows(table_sum[...].astype(LOW), matrix[...])
        grad_pos_queries[pair_rows, :] = summed.astype(LOW)

        @pl.when(lax.rem(pair, 2) == 1)
        def _():
            send_third(pair // 2)

        pair_tasks(pair, 2)
        return carry

    lax.fori_loop(0, width // LANES, pair_back, 0)

    for copy in late_loads:
        copy.wait()

    for part in range(2):
        shift = part * table // 2
        rows = slice(0, table // 2)

        def table_part(rows):
            inside = slice(shift + rows.start, shift + rows.stop)
            turned_dims = (((0,), (1,)), ((), ()))
            summed = lax.dot_general(
                grad_pos_keys[:, inside], weights_in[2], turned_dims, preferred_element_type=F32
            )
            return summed + factor * lax.dot_general(
                grad_pos_queries[:, inside], weights_in[1], turned_dims, preferred_element_type=F32
            )

        place_halves(TABLE_JOBS + part, [rows], table_part)
    run_tasks(("table", 0))
    tokens_grad_low = narrow.at[3]
    for rows in blocks:
        summed = grad_total[rows, :] + factor * dot_rows(grads[0, rows, :], weights_in[1])
        summed = summed + dot_rows(grads[1, rows, :], weights_in[2])
        summed = summed + dot_rows(grads[2, rows, :], weights_in[3])
        tokens_grad_low[rows, :] = summed.astype(LOW)
    mover.leave(tokens_grad_low, tokens_grad)
    run_tasks(("tail", 0))
    exchange.finish()
    for number in range(JOB_COUNT - LEAVING, JOB_COUNT):
        leaving_copy(number).wait_send()
    for step in range(len(vector_partners)):
        vector_copy(step).wait_send()
    mover.finish()


def gradients(
    activation,
    slope,
    in_weights,
    out_weights,
    first_low,
    grad_pre2,
    normed1,
    scale1,
    first_gain,
    output_weight,
    vectors,
    context,
    prob,
    query,
    key,
    value,
    key_table,
    query_table,
    tokens,
    pos_rows,
    query_weight,
    key_weight,
    value_weight,
):
    length, width = tokens.shape
    table = pos_rows.shape[0]
    half = width // 2
    inputs = (
        activation,
        slope,
        in_weights,
        out_weights,
        first_low,
        grad_pre2,
        normed1,
        scale1,
        first_gain,
        output_weight,
        vectors,
        context,
        prob,
        query,
        key,
        value,
        key_table,
        query_table,
        tokens,
        pos_rows,
        query_weight,
        key_weight,
        value_weight,
        jnp.asarray(spread_index(length)),
    )
    anywhere = pl.BlockSpec(memory_space=pl.ANY)
    local = pl.BlockSpec(memory_space=pltpu.VMEM)
    outs = [
        jax.ShapeDtypeStruct((width, 2 * width), LOW),
        jax.ShapeDtypeStruct((2 * width, width), LOW),
        jax.ShapeDtypeStruct((2 * THIRDS, width, half), LOW),
        jax.ShapeDtypeStruct((width, width), LOW),
        jax.ShapeDtypeStruct((table, width), LOW),
        jax.ShapeDtypeStruct((length, width), LOW),
        jax.ShapeDtypeStruct(vectors.shape, F32),
    ]
    slots = TABLE_JOBS + 1
    scratch = [
        pltpu.VMEM((slots, width, half), LOW),
        pltpu.VMEM((slots, width, half), LOW),
        pltpu.VMEM((slots, width // 16 * 15, half), LOW),
        pltpu.VMEM((LEAVING, width, half), LOW),
        pltpu.VMEM((2, 2, length, width), LOW),
        pltpu.VMEM((4, length, width), LOW),
        pltpu.VMEM((4, length, width), LOW),
        pltpu.VMEM((2, 2 * length, width), LOW),
        pltpu.VMEM((4, width, width), LOW),
        pltpu.VMEM((7, width, length), LOW),
        pltpu.VMEM((2, length, length), LOW),
        pltpu.VMEM((length, LANES), F32),
        pltpu.VMEM((LANES, length), F32),
        pltpu.VMEM((LANES, length), F32),
        pltpu.VMEM((LANES, length), F32),
        pltpu.VMEM((LANES, 2 * length), F32),
        pltpu.VMEM((table, 2 * length), LOW),
        pltpu.VMEM((width, table), LOW),
        pltpu.VMEM((width, table), LOW),
        pltpu.VMEM((length, width), F32),
        pltpu.VMEM((length, width), F32),
        pltpu.VMEM((length, 1), F32),
        pltpu.VMEM((2 + PAIR_BITS,) + vectors.shape, F32),
        pltpu.VMEM((1 + PAIR_BITS,) + vectors.shape, F32),
        pltpu.SemaphoreType.DMA((JOB_COUNT, 11)),
        pltpu.SemaphoreType.DMA((JOB_COUNT, 10)),
        pltpu.SemaphoreType.DMA((1 + PAIR_BITS,)),
        pltpu.SemaphoreType.DMA((1 + PAIR_BITS,)),
        pltpu.SemaphoreType.DMA((2,)),
        pltpu.SemaphoreType.DMA((64,)),
    ]
    return pl.pallas_call(
        gradient_kernel,
        in_specs=[local if at in (8, 23) else anywhere for at in range(len(inputs))],
        out_specs=[anywhere] * (len(outs) - 1) + [local],
        out_shape=outs,
        scratch_shapes=scratch,
        compiler_params=pltpu.CompilerParams(
            vmem_limit_bytes=GRADIENT_VMEM_BYTES, collective_id=0, has_side_effects=True
        ),
        name="gradients",
    )(*inputs)


def finish_kernel(
    in_share,
    out_share,
    output_share,
    heads_share,
    table_share,
    position_table,
    output_in,
    tokens_in,
    vectors,
    table_gain,
    in_grad,
    out_grad,
    output_grad,
    query_grad,
    key_grad,
    value_grad,
    table_grad,
    output,
    tokens_grad,
    gain_grad,
    shift_grad,
    *rest,
):
    vector_grads, rest = rest[:4], rest[4:]
    in_low, in_wide, out_low, out_wide, output_low, output_wide, heads_low, *rest = rest
    query_wide, key_wide, value_wide, table_low, table_wide, position_in, *rest = rest
    output_space, tokens_space, sems = rest
    mover = Mover(sems)
    width = output_share.shape[0]
    half = width // 2

    def cuts(source, low, wide, target):
        pieces = []
        for start in range(0, source.shape[0], half):
            rows = pl.ds(start, half)
            pieces.append(
                (mover.start(source.at[rows], low.at[rows]), low, wide, target, rows)
            )
        return pieces

    pieces = cuts(in_share, in_low, in_wide, in_grad)
    pieces += cuts(out_share, out_low, out_wide, out_grad)
    pieces += cuts(output_share, output_low, output_wide, output_grad)
    head_loads = [
        mover.start(heads_share.at[:, pl.ds(start, half)], heads_low.at[:, pl.ds(start, half)])
        for start in range(0, width, half)
    ]
    table_load = mover.start(table_share, table_low)
    position_load = mover.start(position_table, position_in)
    passing = [
        (mover.start(source, space), space, target)
        for source, space, target in (
            (output_in, output_space, output),
            (tokens_in, tokens_space, tokens_grad),
        )
    ]
    for load, low, wide, target, rows in pieces:
        load.wait()
        wide[rows, :] = low[rows, :].astype(F32)
        mover.leave(wide.at[rows], target.at[rows])
    for number, load in enumerate(head_loads):
        load.wait()
        rows = slice(number * half, (number + 1) * half)
        for place, (wide, target) in enumerate(
            ((query_wide, query_grad), (key_wide, key_grad), (value_wide, value_grad))
        ):
            for block in range(2 * THIRDS):
                lanes = slice(place * LANES, (place + 1) * LANES)
                columns = slice(block * LANES, (block + 1) * LANES)
                wide[rows, columns] = heads_low[block, rows, lanes].astype(F32)
            mover.leave(wide.at[rows], target.at[rows])
    for load, space, target in passing:
        load.wait()
        mover.leave(space, target)
    table_load.wait()
    position_load.wait()
    gain = as_row(table_gain)
    grad = table_low[...].astype(F32)
    _, normed, scale_rows = norm_forward(position_in[...].astype(F32), gain, 0.0)
    table_wide[...] = norm_backward(grad, normed, scale_rows, gain)
    mover.leave(table_wide, table_grad)
    gain_grad[...] = jnp.sum(grad * normed, axis=0)
    shift_grad[...] = jnp.sum(grad, axis=0)
    for place, target in enumerate(vector_grads):
        target[...] = vectors[place, :]
    mover.finish()


def finish(shares, vectors, position_table, table_gain, output, tokens_grad):
    in_share, out_share, heads_share, output_share, table_share = shares
    table, width = position_table.shape
    inputs = (
        in_share,
        out_share,
        output_share,
        heads_share,
        table_share,
        position_table,
        output,
        tokens_grad,
        vectors,
        table_gain,
    )
    anywhere = pl.BlockSpec(memory_space=pl.ANY)
    local = pl.BlockSpec(memory_space=pltpu.VMEM)

    def wide(item):
        return jax.ShapeDtypeStruct(item.shape, F32)

    square = jax.ShapeDtypeStruct((width, width), F32)
    vector = jax.ShapeDtypeStruct((width,), F32)
    outs = [wide(in_share), wide(out_share), square, square, square, square, wide(table_share)]
    outs += [jax.ShapeDtypeStruct(item.shape, LOW) for item in (output, tokens_grad)]
    outs += [vector] * 6
    scratch = []
    for item in (in_share, out_share, output_share):
        scratch += [pltpu.VMEM(item.shape, LOW), pltpu.VMEM(item.shape, F32)]
    scratch += [pltpu.VMEM(heads_share.shape, LOW)] + [pltpu.VMEM((width, width), F32)] * 3
    scratch += [pltpu.VMEM((table, width), LOW), pltpu.VMEM((table, width), F32)]
    scratch += [pltpu.VMEM(item.shape, LOW) for item in (position_table, output, tokens_grad)]
    scratch.append(pltpu.SemaphoreType.DMA((64,)))
    return pl.pallas_call(
        finish_kernel,
        in_specs=[anywhere] * 8 + [local] * 2,
        out_specs=[anywhere] * 9 + [local] * 6,
        out_shape=outs,
        scratch_shapes=scratch,
        compiler_params=pltpu.CompilerParams(vmem_limit_bytes=VMEM_BYTES),
        name="finish",
    )(*inputs)


def beyond(shares):
    in_share, out_share, *others = shares
    chips = 1 << PAIR_BITS
    rows, columns = lax.axis_size("rows"), lax.axis_size("cols")
    if rows > chips:
        groups = [[at + chips * step for step in range(rows // chips)] for at in range(chips)]
        in_share, out_share, *others = lax.psum(
            (in_share, out_share, *others), "rows", axis_index_groups=groups
        )
    if columns > 2:
        groups = [[at + 2 * step for step in range(columns // 2)] for at in range(2)]
        others = lax.psum(tuple(others), "cols", axis_index_groups=groups)
        in_share = lax.psum_scatter(
            in_share, "cols", scatter_dimension=1, axis_index_groups=groups, tiled=True
        )
        out_share = lax.psum_scatter(
            out_share, "cols", scatter_dimension=0, axis_index_groups=groups, tiled=True
        )
    return (in_share, out_share, *others)


def on_device(
    tokens,
    segment_ids,
    position_table,
    table_gain,
    table_shift,
    query_weight,
    key_weight,
    value_weight,
    output_weight,
    first_gain,
    first_shift,
    feedforward_input_weight,
    ffn_out,
    second_gain,
    second_shift,
    out_grad,
):
    (
        query,
        key,
        value,
        prob,
        context,
        normed1,
        scale1,
        first_low,
        key_table,
        query_table,
        pos_rows,
        in_weights,
        out_weights,
        activation,
        slope,
        grad_pre2,
        output,
        vectors,
    ) = forward(
        tokens,
        segment_ids,
        position_table,
        table_gain,
        table_shift,
        query_weight,
        key_weight,
        value_weight,
        output_weight,
        first_gain,
        first_shift,
        feedforward_input_weight,
        ffn_out,
        second_gain,
        second_shift,
        out_grad,
    )
    shares = gradients(
        activation,
        slope,
        in_weights,
        out_weights,
        first_low,
        grad_pre2,
        normed1,
        scale1,
        first_gain,
        output_weight,
        vectors,
        context,
        prob,
        query,
        key,
        value,
        key_table,
        query_table,
        tokens,
        pos_rows,
        query_weight,
        key_weight,
        value_weight,
    )
    *sums, vectors = beyond(shares[:5] + shares[6:])
    (
        in_grad,
        out_weight_grad,
        output_weight_grad,
        query_grad,
        key_grad,
        value_grad,
        table_grad,
        output,
        tokens_grad,
        table_gain_grad,
        table_shift_grad,
        second_gain_grad,
        second_shift_grad,
        first_gain_grad,
        first_shift_grad,
    ) = finish(sums, vectors, position_table, table_gain, output, shares[5])
    return (
        output,
        tokens_grad,
        table_grad,
        table_gain_grad,
        table_shift_grad,
        query_grad,
        key_grad,
        value_grad,
        output_weight_grad,
        first_gain_grad,
        first_shift_grad,
        in_grad,
        out_weight_grad,
        second_gain_grad,
        second_shift_grad,
    )


def solution(mesh):
    spread = P(("rows", "cols"), None)
    in_specs = (spread, spread) + (P(),) * 9 + (P(None, "cols"), P("cols", None), P(), P(), spread)
    out_specs = (
        (spread, spread) + (P(),) * 9 + (P(None, "cols"), P("cols", None), P(), P())
    )
    return jax.shard_map(
        on_device, mesh=mesh, in_specs=in_specs, out_specs=out_specs, check_vma=False
    )
```

```python
import math

import jax
import jax.numpy as jnp
import numpy as np
from jax import lax
from jax.experimental import pallas as pl
from jax.experimental.pallas import tpu as pltpu
from jax.sharding import PartitionSpec as P

HEAD_DIM = 64
BUCKETS = 256
MAX_POS = 512
EPSILON = 1e-07
NEGATIVE = -1e30
ROOT_HALF = 0.7071067811865476
DENSITY_SCALE = 0.3989422804014327
LOG2_E = 1.4426950408889634

LANES = 128
VMEM_BYTES = 56 * 1024 * 1024
GRADIENT_VMEM_BYTES = 60 * 1024 * 1024
F32 = jnp.float32
LOW = jnp.bfloat16


def bucket_table(length):
    middle = BUCKETS // 2
    distance = np.arange(-(length - 1), length)
    direction = np.sign(distance)
    magnitude = np.where((distance < middle) & (distance > -middle), middle - 1, np.abs(distance))
    logged = (
        np.ceil(np.log(magnitude / middle) / np.log((MAX_POS - 1) / middle) * (middle - 1)) + middle
    )
    bucket = np.where(magnitude <= middle, distance, logged * direction)
    return np.clip(bucket + BUCKETS, 0, 2 * BUCKETS - 1).astype(np.int32)


def spread_index(length):
    table = np.concatenate([bucket_table(length)[::-1], [-1]]).astype(np.int32)
    return table.reshape(1, 2 * length)


def dot(left, right):
    return jnp.dot(left, right, preferred_element_type=F32)


def dot_rows(left, right):
    return lax.dot_general(left, right, (((1,), (1,)), ((), ())), preferred_element_type=F32)


def dot_columns(left, right):
    return lax.dot_general(left, right, (((0,), (0,)), ((), ())), preferred_element_type=F32)


def norm_forward(value, gain, shift):
    centered = value - jnp.mean(value, axis=-1, keepdims=True)
    squared_spread = jnp.mean(centered * centered, axis=-1, keepdims=True)
    scale_rows = lax.rsqrt(squared_spread + EPSILON)
    normed = centered * scale_rows
    return (normed * gain + shift, normed, scale_rows)


def norm_backward(grad, normed, scale_rows, gain):
    scaled = grad * gain
    return scale_rows * (
        scaled
        - jnp.mean(scaled, axis=-1, keepdims=True)
        - normed * jnp.mean(scaled * normed, axis=-1, keepdims=True)
    )


def pair_columns(pair):
    return pl.ds(pl.multiple_of(pair * LANES, LANES), LANES)


def head_lanes(rows, half):
    lane = lax.broadcasted_iota(jnp.int32, (rows, LANES), 1)
    return (lane < HEAD_DIM) if half == 0 else (lane >= HEAD_DIM)


def spread_columns(index_ref, buckets):
    column = lax.broadcasted_iota(jnp.int32, (index_ref.shape[0], buckets), 1)
    return jnp.where(index_ref[...] == column, 1.0, 0.0).astype(LOW)


def spread_matrix(index_ref, buckets):
    row = lax.broadcasted_iota(jnp.int32, (buckets, index_ref.shape[1]), 0)
    return jnp.where(index_ref[...] == row, 1.0, 0.0).astype(LOW)


def flip_matrix():
    row = lax.broadcasted_iota(jnp.int32, (LANES, LANES), 0)
    column = lax.broadcasted_iota(jnp.int32, (LANES, LANES), 1)
    return jnp.where(row + column == LANES - 1, 1.0, 0.0).astype(LOW)


def unit_matrix():
    row = lax.broadcasted_iota(jnp.int32, (LANES, LANES), 0)
    column = lax.broadcasted_iota(jnp.int32, (LANES, LANES), 1)
    return jnp.where(row == column, 1.0, 0.0).astype(LOW)


def both_heads(pair_rows):
    rows = pair_rows.shape[0]
    return jnp.concatenate(
        [jnp.where(head_lanes(rows, half), pair_rows, 0) for half in range(2)], axis=0
    )


def join_heads(stacked):
    rows = stacked.shape[0] // 2
    return jnp.where(head_lanes(rows, 0), stacked[:rows], stacked[rows:])


def tiles_of(value):
    return [value[:, at : at + LANES] for at in range(0, value.shape[1], LANES)]


def turn(tile, first):
    return pltpu.roll(tile, first, 1, stride=1, stride_axis=0)


def lane_from(distance):
    row = lax.broadcasted_iota(jnp.int32, (LANES, LANES), 0)
    lane = lax.broadcasted_iota(jnp.int32, (LANES, LANES), 1)
    return lane >= row + distance


def skewed(window, length):
    turned = [turn(tile, 1) for tile in tiles_of(window)]
    late = lane_from(1)
    parts = [jnp.where(late, after, tile) for tile, after in zip(turned, turned[1:])]
    return jnp.concatenate(parts, axis=1)


def unskewed(flipped):
    turned = [turn(tile, 0) for tile in tiles_of(flipped)]
    late = lane_from(0)
    nothing = jnp.zeros_like(turned[0])
    before, after = [nothing] + turned, turned + [nothing]
    parts = [jnp.where(late, tile, left) for left, tile in zip(before, after)]
    return jnp.concatenate(parts, axis=1)


def as_row(vector):
    return vector[...].reshape(1, vector.shape[0])


def whole(shape):
    zeros = (0,) * len(shape)
    return pl.BlockSpec(shape, lambda *_: zeros, pipeline_mode=pl.Buffered(1))


def whole_out(shape):
    zeros = (0,) * len(shape)
    return pl.BlockSpec(shape, lambda *_: zeros)


def gelu_parts(value):
    divisor = 1.0 + (0.3275911 * ROOT_HALF) * jnp.abs(value)
    guess = pl.reciprocal(divisor, approx=True)
    part = guess * (2.0 - divisor * guess)
    part = part * (2.0 - divisor * part)
    bell = jnp.exp2((-0.5 * LOG2_E) * (value * value))
    series = (0.5 * 1.061405429) * part - (0.5 * 1.453152027)
    series = series * part + (0.5 * 1.421413741)
    series = series * part - (0.5 * 0.284496736)
    series = series * part + (0.5 * 0.254829592)
    tail = series * (part * bell)
    return jnp.where(value < 0.0, tail, 1.0 - tail), (DENSITY_SCALE * value) * bell


class Mover:
    def __init__(self, sems):
        self.sems, self.count, self.open = sems, 0, []

    def start(self, source, target):
        copy = pltpu.make_async_copy(source, target, self.sems.at[self.count])
        self.count += 1
        copy.start()
        return copy

    def leave(self, source, target):
        self.open.append(self.start(source, target))

    def finish(self):
        for copy in self.open:
            copy.wait()


def unit_order(parts):
    return [(place % (parts // 2)) * 2 + place // (parts // 2) for place in range(parts)]


def forward_kernel(
    tokens,
    segments,
    table,
    table_gain,
    table_shift,
    query_weight,
    key_weight,
    value_weight,
    output_weight,
    first_gain,
    first_shift,
    in_weight,
    out_weight,
    second_gain,
    second_shift,
    out_grad,
    spread,
    query_out,
    key_out,
    value_out,
    prob_out,
    context_out,
    normed_out,
    scale_out,
    first_low_out,
    key_table_out,
    query_table_out,
    pos_rows_out,
    in_weights_out,
    out_weights_out,
    activation_out,
    slope_out,
    grad_pre2_out,
    output_out,
    vectors_out,
    tokens_in,
    table_in,
    weights_in,
    out_grad_in,
    heads_in,
    tables_in,
    pos_rows_in,
    probs,
    context,
    normed,
    scale,
    first_low,
    total,
    in_weights,
    out_weights,
    inner,
    activation,
    slope,
    output,
    vectors,
    mask,
    crossed,
    send_sems,
    receive_sems,
    prob_sems,
    move_sems,
):
    length, width = tokens.shape
    parts, _, units = in_weights.shape
    factor = 1.0 / math.sqrt(3 * HEAD_DIM)
    row, me = lax.axis_index("rows"), lax.axis_index("cols")
    mover = Mover(move_sems)
    table_load = mover.start(table, table_in)
    key_load = mover.start(key_weight, weights_in.at[1])
    query_load = mover.start(query_weight, weights_in.at[0])
    tokens_load = mover.start(tokens, tokens_in)
    value_load = mover.start(value_weight, weights_in.at[2])
    output_load = mover.start(output_weight, weights_in.at[3])
    grad_load = mover.start(out_grad, out_grad_in)
    own_loads = [
        mover.start(in_weight, in_weights.at[me]),
        mover.start(out_weight, out_weights.at[me]),
    ]
    peers = [lax.rem(me + step, parts) for step in range(1, parts)]
    barrier = pltpu.get_barrier_semaphore()
    for peer in peers:
        pl.semaphore_signal(
            barrier, inc=1, device_id=(row, peer), device_id_type=pl.DeviceIdType.MESH
        )
    pl.semaphore_wait(barrier, parts - 1)

    def shard_copy(kind, step, place):
        source, target = ((in_weight, in_weights), (out_weight, out_weights))[kind]
        return pltpu.make_async_remote_copy(
            src_ref=source,
            dst_ref=target.at[place],
            send_sem=send_sems.at[kind, step],
            recv_sem=receive_sems.at[kind, step],
            device_id=(row, peers[step]),
            device_id_type=pl.DeviceIdType.MESH,
        )

    for kind in range(2):
        for step in range(parts - 1):
            shard_copy(kind, step, me).start()

    key_load.wait()
    query_load.wait()
    table_load.wait()
    pos_out, _, _ = norm_forward(table_in[...].astype(F32), as_row(table_gain), as_row(table_shift))
    pos_rows_in[...] = pos_out.astype(LOW)
    mover.leave(pos_rows_in, pos_rows_out)
    matrix = spread_columns(spread, table.shape[0])
    pos_keys = dot(pos_rows_in[...], weights_in[1]).astype(LOW)
    tables_in[0] = dot(matrix, pos_keys).astype(LOW)
    pos_queries = (dot(pos_rows_in[...], weights_in[0]) * factor).astype(LOW)
    tables_in[1] = dot(matrix, pos_queries).astype(LOW)
    mover.leave(tables_in.at[0], key_table_out)
    mover.leave(tables_in.at[1], query_table_out)
    tokens_load.wait()
    heads_in[0] = (dot(tokens_in[...], weights_in[0]) * factor).astype(LOW)
    heads_in[1] = dot(tokens_in[...], weights_in[1]).astype(LOW)
    value_load.wait()
    heads_in[2] = dot(tokens_in[...], weights_in[2]).astype(LOW)
    for place, target in enumerate((query_out, key_out, value_out)):
        mover.leave(heads_in.at[place], target)
    document = lax.broadcasted_iota(jnp.int32, (8, length), 0)
    member = jnp.where(segments[...] == document, 1.0, 0.0).astype(LOW)
    mask[...] = jnp.where(dot_columns(member, member) > 0.5, 0.0, NEGATIVE)

    blocks = [slice(at * LANES, (at + 1) * LANES) for at in range(length // LANES)]
    unit = unit_matrix()

    pairs = width // LANES

    def prob_copy(pair):
        heads = pl.ds(2 * pair, 2)
        return pltpu.make_async_copy(probs.at[heads], prob_out.at[heads], prob_sems.at[pair])

    def one_pair(pair, carry):
        columns = pair_columns(pair)
        query_pair = heads_in[0, :, columns]
        key_pair = heads_in[1, :, columns]
        value_pair = heads_in[2, :, columns]
        for rows in blocks:
            start = length - rows.stop
            keys = both_heads(key_pair[rows])
            window = dot_rows(keys, tables_in[1, start : start + length + LANES, columns])
            for half in range(2):
                part = window[half * LANES : (half + 1) * LANES]
                crossed[half, rows, :] = skewed(part, length).astype(LOW)
        for rows in blocks:
            start = length - rows.stop
            queries = both_heads(query_pair[rows])
            window = dot_rows(queries, tables_in[0, start : start + length + LANES, columns])
            for half in range(2):
                span = slice(half * LANES, (half + 1) * LANES)
                left = jnp.concatenate([queries[span], unit], axis=1)
                right = jnp.concatenate([key_pair, crossed[half, :, rows]], axis=1)
                scores = dot_rows(left, right) + skewed(window[span], length) + mask[rows, :]
                top = jnp.max(scores, axis=-1, keepdims=True)
                weights = jnp.exp(scores - top)
                share = jnp.sum(weights, axis=-1, keepdims=True)
                probs[2 * pair + half, rows, :] = (weights * (1.0 / share)).astype(LOW)
        contexts = [dot(probs[2 * pair + half], value_pair) for half in range(2)]
        joined = jnp.where(head_lanes(length, 0), contexts[0], contexts[1])
        context[:, columns] = joined.astype(LOW)
        prob_copy(pair).start()
        return carry

    lax.fori_loop(0, pairs, one_pair, 0)
    mover.leave(context, context_out)

    output_load.wait()
    halves = [slice(at, at + length // 2) for at in range(0, length, length // 2)]
    for rows in halves:
        pre = dot(context[rows, :], weights_in[3]) + tokens_in[rows, :].astype(F32)
        first, first_normed, scale_rows = norm_forward(pre, as_row(first_gain), as_row(first_shift))
        total[rows, :] = first
        first_low[rows, :] = first.astype(LOW)
        normed[rows, :] = first_normed
        scale[rows, :] = scale_rows
    mover.leave(first_low, first_low_out)
    mover.leave(normed, normed_out)
    mover.leave(scale, scale_out)

    for copy in own_loads:
        copy.wait()
    for kind in range(2):
        for step in range(parts - 1):
            shard_copy(kind, step, lax.rem(me + parts - 1 - step, parts)).wait_recv()
    mover.leave(in_weights, in_weights_out)
    mover.leave(out_weights, out_weights_out)
    size = math.gcd(units, width)
    chunks = [
        (part, slice(at, at + size)) for part in unit_order(parts) for at in range(0, units, size)
    ]

    def begin(number, rows):
        part, cut = chunks[number]
        inner[number % 2, rows, :] = dot(first_low[rows, :], in_weights[part, :, cut])

    for rows in halves:
        begin(0, rows)
    for number, (part, cut) in enumerate(chunks):
        columns = slice(number * size, (number + 1) * size)
        for rows in halves:
            if number + 1 < len(chunks):
                begin(number + 1, rows)
            value = inner[number % 2, rows, :]
            cumulative, bent = gelu_parts(value)
            activation[rows, columns] = (value * cumulative).astype(LOW)
            slope[rows, columns] = (cumulative + bent).astype(LOW)
            total[rows, :] += dot(activation[rows, columns], out_weights[part, cut, :])
        mover.leave(activation.at[:, columns], activation_out.at[:, columns])
        mover.leave(slope.at[:, columns], slope_out.at[:, columns])
    grad_load.wait()
    gain_sum = jnp.zeros((1, width), F32)
    shift_sum = jnp.zeros((1, width), F32)
    for rows in halves:
        second, second_normed, scale_rows = norm_forward(
            total[rows, :], as_row(second_gain), as_row(second_shift)
        )
        output[rows, :] = second.astype(LOW)
        grad_out = out_grad_in[rows, :].astype(F32)
        gain_sum = gain_sum + jnp.sum(grad_out * second_normed, axis=0, keepdims=True)
        shift_sum = shift_sum + jnp.sum(grad_out, axis=0, keepdims=True)
        total[rows, :] = norm_backward(grad_out, second_normed, scale_rows, as_row(second_gain))
    mover.leave(total, grad_pre2_out)
    mover.leave(output, output_out)
    vectors[0:1, :] = gain_sum
    vectors[1:2, :] = shift_sum
    vectors[2:8, :] = jnp.zeros((6, width), F32)
    mover.leave(vectors, vectors_out)
    for kind in range(2):
        for step in range(parts - 1):
            shard_copy(kind, step, me).wait_send()
    for pair in range(pairs):
        prob_copy(pair).wait()
    mover.finish()


def forward(
    tokens,
    segment_ids,
    table,
    table_gain,
    table_shift,
    query_weight,
    key_weight,
    value_weight,
    output_weight,
    first_gain,
    first_shift,
    in_weight,
    out_weight,
    second_gain,
    second_shift,
    out_grad,
):
    length, width = tokens.shape
    heads = width // HEAD_DIM
    parts, units = lax.axis_size("cols"), in_weight.shape[1]
    hidden = parts * units
    chunk = math.gcd(units, width)
    inputs = (
        tokens,
        segment_ids,
        table,
        table_gain,
        table_shift,
        query_weight,
        key_weight,
        value_weight,
        output_weight,
        first_gain,
        first_shift,
        in_weight,
        out_weight,
        second_gain,
        second_shift,
        out_grad,
        jnp.asarray(spread_index(length).reshape(2 * length, 1)),
    )
    anywhere = pl.BlockSpec(memory_space=pl.ANY)
    local = pl.BlockSpec(memory_space=pltpu.VMEM)
    in_specs = [local if at in (1, 3, 4, 9, 10, 13, 14, 16) else anywhere for at in range(17)]

    def low(*shape):
        return jax.ShapeDtypeStruct(shape, LOW)

    def wide(*shape):
        return jax.ShapeDtypeStruct(shape, F32)

    outs = [
        low(length, width),
        low(length, width),
        low(length, width),
        low(heads, length, length),
        low(length, width),
        wide(length, width),
        wide(length, 1),
        low(length, width),
        low(2 * length, width),
        low(2 * length, width),
        low(*table.shape),
        low(parts, width, units),
        low(parts, units, width),
        low(length, hidden),
        low(length, hidden),
        wide(length, width),
        low(length, width),
        wide(8, width),
    ]
    scratch = [
        pltpu.VMEM((length, width), LOW),
        pltpu.VMEM(table.shape, LOW),
        pltpu.VMEM((4, width, width), LOW),
        pltpu.VMEM((length, width), LOW),
        pltpu.VMEM((3, length, width), LOW),
        pltpu.VMEM((2, 2 * length, width), LOW),
        pltpu.VMEM(table.shape, LOW),
        pltpu.VMEM((heads, length, length), LOW),
        pltpu.VMEM((length, width), LOW),
        pltpu.VMEM((length, width), F32),
        pltpu.VMEM((length, 1), F32),
        pltpu.VMEM((length, width), LOW),
        pltpu.VMEM((length, width), F32),
        pltpu.VMEM((parts, width, units), LOW),
        pltpu.VMEM((parts, units, width), LOW),
        pltpu.VMEM((2, length, chunk), F32),
        pltpu.VMEM((length, hidden), LOW),
        pltpu.VMEM((length, hidden), LOW),
        pltpu.VMEM((length, width), LOW),
        pltpu.VMEM((8, width), F32),
        pltpu.VMEM((length, length), F32),
        pltpu.VMEM((2, length, length), LOW),
        pltpu.SemaphoreType.DMA((2, parts - 1)),
        pltpu.SemaphoreType.DMA((2, parts - 1)),
        pltpu.SemaphoreType.DMA((heads // 2,)),
        pltpu.SemaphoreType.DMA((24 + 2 * (hidden // chunk),)),
    ]
    return pl.pallas_call(
        forward_kernel,
        in_specs=in_specs,
        out_specs=[anywhere] * len(outs),
        out_shape=outs,
        scratch_shapes=scratch,
        compiler_params=pltpu.CompilerParams(
            vmem_limit_bytes=VMEM_BYTES, collective_id=1, has_side_effects=True
        ),
        name="forward",
    )(*inputs)


def split_flip(matrix, value):
    high = value.astype(LOW)
    rest = (value - high.astype(F32)).astype(LOW)
    return dot(matrix, high) + dot(matrix, rest)


PAIR_BITS = 4
TABLE_JOBS = 12
JOB_COUNT = 14
LEAVING = 3
THIRDS = 3
ORDERS = (
    (0, 2, 1, 3),
    (1, 2, 0, 3),
    (0, 1, 2, 3),
    (1, 0, 2, 3),
    (2, 0, 1, 3),
    (2, 1, 0, 3),
    (0, 2, 3, 1),
    (1, 2, 3, 0),
)
COLOURS = (5, 1, 2, 2, 1, 4, 4, 3, 0, 1, 2, 3, 4, 2)
TASKS_AFTER = {
    ("out", 1): (
        (0, 0), (1, 0),
    ),
    ("in", 0): (
        (2, 0),
    ),
    ("in", 1): (
        (4, 0), (3, 0), (5, 0),
    ),
    ("norm", 0): (
        (0, 1), (1, 1), (14, 0),
    ),
    ("context", 0): (
        (7, 0), (14, 1),
    ),
    ("prepare", 0): (
        (5, 1), (14, 2),
    ),
    ("head", 0): (
        (4, 1), (6, 0),
    ),
    ("head", 1): (
        (8, 0),
    ),
    ("head", 2): (
        (14, 3),
    ),
    ("head", 4): (
        (3, 1), (5, 2), (14, 4),
    ),
    ("head", 6): (
        (4, 2), (14, 5),
    ),
    ("head", 8): (
        (1, 2), (0, 2), (2, 1), (8, 1), (7, 1),
    ),
    ("head", 9): (
        (4, 3), (5, 3), (9, 0), (3, 2),
    ),
    ("head", 12): (
        (4, 4), (2, 2),
    ),
    ("head", 13): (
        (0, 3), (7, 2), (10, 0),
    ),
    ("head", 15): (
        (1, 3), (4, 5),
    ),
    ("head", 16): (
        (9, 1), (8, 2), (3, 3),
    ),
    ("head", 17): (
        (6, 1), (7, 3),
    ),
    ("table", 0): (
        (8, 3), (11, 0), (12, 0), (3, 4), (4, 6), (0, 4), (6, 2), (7, 4), (13, 0), (8, 4),
        (3, 5), (9, 2), (5, 4), (0, 5), (10, 1), (6, 3), (8, 5), (1, 4), (12, 1), (7, 5),
        (5, 5), (11, 1), (9, 3), (12, 2), (3, 6), (6, 4), (13, 1), (10, 2), (5, 6), (9, 4),
        (7, 6), (4, 7), (11, 2), (12, 3), (10, 3), (9, 5), (8, 6), (11, 3), (6, 5), (1, 5),
        (0, 6), (3, 7), (10, 4), (11, 4), (13, 2), (10, 5), (9, 6), (12, 4), (13, 3),
        (7, 7), (2, 3),
    ),
    ("tail", 0): (
        (12, 5), (8, 7), (11, 5), (2, 4), (1, 6), (13, 4), (10, 6), (9, 7), (0, 7), (6, 6),
        (11, 6), (12, 6), (2, 5), (13, 5), (13, 6), (8, 8), (12, 7), (2, 6), (10, 7),
        (11, 7), (13, 7), (6, 7), (2, 7), (9, 8), (7, 8), (12, 8), (8, 9), (1, 7), (5, 7),
        (3, 8), (10, 8), (13, 8), (9, 9), (4, 8), (12, 9), (13, 9), (0, 8), (11, 8), (6, 8),
        (11, 9), (2, 8), (10, 9), (5, 8), (1, 8),
    ),
}


class Job:
    def __init__(self, number, rows, colour, slot, lift, gathered):
        self.number, self.rows, self.colour = number, rows, colour
        self.slot, self.lift, self.gathered = slot, lift, gathered

    def received(self, stage):
        start = sum(self.rows >> (step + 1) for step in range(stage))
        return (self.lift // 16 * 15) + start, self.rows >> (stage + 1)


def make_jobs(height, table):
    jobs = [Job(n, height, COLOURS[n], n, 0, n >= 8) for n in range(TABLE_JOBS)]
    jobs.append(Job(TABLE_JOBS, table // 2, COLOURS[TABLE_JOBS], TABLE_JOBS, 0, True))
    jobs.append(Job(TABLE_JOBS + 1, table // 2, COLOURS[TABLE_JOBS + 1], TABLE_JOBS, table // 2, True))
    return jobs


class Exchange:
    def __init__(self, partial, landed, received, send_sems, receive_sems, outs, jobs):
        self.partial, self.landed, self.received = partial, landed, received
        self.send_sems, self.receive_sems = send_sems, receive_sems
        self.outs, self.jobs = outs, jobs
        row, column = lax.axis_index("rows"), lax.axis_index("cols")
        self.core = column % 2
        self.twin = (row, column + 1 - 2 * self.core)
        self.bits = [(row // (1 << bit)) % 2 for bit in range(PAIR_BITS)]
        self.partners = [
            (row + (1 - 2 * self.bits[bit]) * (1 << bit), column) for bit in range(PAIR_BITS)
        ]
        self.spans = {}
        for rows, colour in sorted({(job.rows, job.colour) for job in jobs}):
            base, size, kept, sent = 0, rows, [], []
            for bit in ORDERS[colour]:
                size //= 2
                sent.append((base + (1 - self.bits[bit]) * size, size))
                base = base + self.bits[bit] * size
                kept.append((base, size))
            self.spans[rows, colour] = (kept, sent)

    def greet(self):
        barrier = pltpu.get_barrier_semaphore()
        for partner in [self.twin] + self.partners:
            pl.semaphore_signal(
                barrier, inc=1, device_id=partner, device_id_type=pl.DeviceIdType.MESH
            )
        pl.semaphore_wait(barrier, 1 + PAIR_BITS)

    def copy(self, job, stage, source, target, partner):
        return pltpu.make_async_remote_copy(
            src_ref=source,
            dst_ref=target,
            send_sem=self.send_sems.at[job.number, stage],
            recv_sem=self.receive_sems.at[job.number, stage],
            device_id=partner,
            device_id_type=pl.DeviceIdType.MESH,
        )

    def rows_of(self, job, span):
        start, size = span
        return pl.ds(pl.multiple_of(job.lift + start, 16), size)

    def stage(self, job, stage):
        kept, sent = self.spans[job.rows, job.colour]
        order = ORDERS[job.colour]
        if stage < 4:
            source = self.partial.at[job.slot, self.rows_of(job, sent[stage])]
            start, size = job.received(stage)
            target = self.received.at[job.slot, pl.ds(start, size)]
            return self.copy(job, stage, source, target, self.partners[order[stage]])
        if stage < 8:
            source = self.landed.at[job.slot, self.rows_of(job, kept[7 - stage])]
            return self.copy(job, stage, source, source, self.partners[order[7 - stage]])
        rows = pl.ds(job.lift, job.rows)
        return self.copy(
            job, stage, self.landed.at[job.slot, rows], self.outs[job.number], self.twin
        )

    def arrival(self, job, stage):
        kept, sent = self.spans[job.rows, job.colour]
        if 4 <= stage < 8:
            target = self.landed.at[job.slot, self.rows_of(job, sent[7 - stage])]
            order = ORDERS[job.colour]
            return self.copy(job, stage, target, target, self.partners[order[7 - stage]])
        return self.stage(job, stage)

    def twin_copy(self, job, source):
        target = self.landed.at[job.slot, pl.ds(job.lift, job.rows)]
        return self.copy(job, 9, source, target, self.twin)

    def keep_copy(self, job):
        return pltpu.make_async_copy(
            self.landed.at[job.slot, pl.ds(job.lift, job.rows)],
            self.outs[job.number],
            self.send_sems.at[job.number, 10],
        )

    def run(self, number, task):
        job = self.jobs[number]
        kept, _ = self.spans[job.rows, job.colour]
        if task == 0:
            rows = pl.ds(job.lift, job.rows)
            self.twin_copy(job, self.landed.at[job.slot, rows]).wait_recv()
            self.partial[job.slot, rows, :] += self.landed[job.slot, rows, :]
        elif task <= 4:
            self.arrival(job, task - 1).wait_recv()
            start, size = job.received(task - 1)
            rows = self.rows_of(job, kept[task - 1])
            total = self.partial[job.slot, rows, :] + self.received[job.slot, pl.ds(start, size), :]
            if task < 4:
                self.partial[job.slot, rows, :] = total
            else:
                self.landed[job.slot, rows, :] = total
        elif task <= 8:
            self.arrival(job, task - 1).wait_recv()
        if task < 8:
            self.stage(job, task).start()
        elif task == 8:
            self.keep_copy(job).start()
            if job.gathered:
                self.stage(job, 8).start()
        else:
            self.arrival(job, 8).wait_recv()

    def finish(self):
        for job in self.jobs:
            for stage in range(8):
                self.stage(job, stage).wait_send()
            if job.gathered:
                self.stage(job, 8).wait_send()
            self.keep_copy(job).wait()


def gradient_kernel(
    activation,
    slope,
    in_weights,
    out_weights,
    first_low,
    grad_pre2,
    normed1,
    scale1,
    first_gain,
    output_weight,
    vectors,
    context,
    prob,
    query,
    key,
    value,
    key_table,
    query_table,
    tokens,
    pos_rows,
    query_weight,
    key_weight,
    value_weight,
    spread,
    in_share,
    out_share,
    heads_share,
    output_share,
    table_share,
    tokens_grad,
    vector_sums,
    partial,
    landed,
    received,
    leaving,
    hidden,
    narrow,
    heads_in,
    tables_in,
    weights_in,
    turned,
    grad_scores,
    flip_sums,
    key_turned_sum,
    query_turned_sum,
    value_turned_sum,
    table_sum,
    matrix,
    grad_pos_keys,
    grad_pos_queries,
    grad_total,
    normed_in,
    scale_in,
    vector_steps,
    vector_received,
    send_sems,
    receive_sems,
    vector_send_sems,
    vector_receive_sems,
    prob_sems,
    load_sems,
):
    length, width = tokens.shape
    parts, _, units = in_weights.shape
    table = pos_rows.shape[0]
    half = width // 2
    factor = 1.0 / math.sqrt(3 * HEAD_DIM)
    core = lax.axis_index("cols") % 2
    own = pl.multiple_of(core * half, half)
    jobs = make_jobs(width, table)
    outs = []
    for chunk in range(2):
        for part in range(2):
            outs.append(out_share.at[pl.ds(chunk * width, width), pl.ds(part * half, half)])
    for chunk in range(2):
        for part in range(2):
            outs.append(in_share.at[:, pl.ds(chunk * width + part * half, half)])
    outs.append(output_share.at[:, pl.ds(own, half)])
    for third in range(THIRDS):
        outs.append(heads_share.at[2 * third + core])
    for part in range(2):
        outs.append(table_share.at[pl.ds(part * table // 2, table // 2), pl.ds(own, half)])
    exchange = Exchange(partial, landed, received, send_sems, receive_sems, outs, jobs)
    mover = Mover(load_sems)

    sides = ((1 - core, 0), (core, 0), (1 - core, 1), (core, 1))

    def hidden_columns(number):
        side, chunk = sides[number]
        return pl.ds(pl.multiple_of(side * 2 * width + chunk * width, width), width)

    def load_weights(number):
        side, chunk = sides[number]
        piece = min(units, width)
        copies = []
        for start in range(0, width, piece):
            unit = chunk * width + start
            part, offset = 2 * (unit // units) + side, unit % units
            inside = pl.ds(start, piece)
            copies.append(
                mover.start(
                    out_weights.at[part, pl.ds(offset, piece)],
                    weights_in.at[2 + number % 2, inside],
                )
            )
            copies.append(
                mover.start(
                    in_weights.at[part, :, pl.ds(offset, piece)],
                    weights_in.at[number % 2, :, inside],
                )
            )
        return copies

    def load_hidden(source, number, slot):
        return mover.start(source.at[:, hidden_columns(number)], hidden.at[slot // 2, slot % 2])

    total_load = mover.start(grad_pre2, grad_total)
    active_loads = [load_hidden(activation, number, number) for number in range(4)]
    first_load = mover.start(first_low, narrow.at[0])
    weight_loads = [load_weights(number) for number in range(2)]
    vector_load = mover.start(vectors, vector_steps.at[0])
    norm_loads = (mover.start(normed1, normed_in), mover.start(scale1, scale_in))
    context_load = mover.start(context, narrow.at[2])
    head_loads = [
        mover.start(item, heads_in.at[place]) for place, item in enumerate((query, key, value))
    ]
    head_loads += [
        mover.start(key_table, tables_in.at[0]),
        mover.start(query_table, tables_in.at[1]),
    ]
    exchange.greet()

    def run_tasks(name):
        for number, task in TASKS_AFTER.get(name, ()):
            if number < JOB_COUNT:
                exchange.run(number, task)
            else:
                vector_task(task)

    vector_partners = [exchange.twin] + exchange.partners

    def vector_copy(step):
        return pltpu.make_async_remote_copy(
            src_ref=vector_steps.at[step],
            dst_ref=vector_received.at[step],
            send_sem=vector_send_sems.at[step],
            recv_sem=vector_receive_sems.at[step],
            device_id=vector_partners[step],
            device_id_type=pl.DeviceIdType.MESH,
        )

    def vector_task(step):
        if step > 0:
            vector_copy(step - 1).wait_recv()
            vector_steps[step] = vector_steps[step - 1] + vector_received[step - 1]
        if step < len(vector_partners):
            vector_copy(step).start()
        else:
            vector_sums[...] = vector_steps[step]

    def leaving_copy(number):
        job = jobs[number]
        return exchange.twin_copy(job, leaving.at[number % LEAVING, pl.ds(0, job.rows)])

    def open_space(number):
        if number >= LEAVING:
            leaving_copy(number - LEAVING).wait_send()
        return leaving.at[number % LEAVING, pl.ds(0, jobs[number].rows)]

    lower = [slice(0, half), slice(half, width)]

    def place_hidden(side, number, part_of):
        if side == 0:
            targets = [open_space(number), open_space(number + 1)]
        else:
            targets = [partial.at[number], partial.at[number + 1]]
        for rows in lower:
            value = part_of(rows).astype(LOW)
            for target, columns in zip(targets, lower):
                target[rows, :] = value[:, columns]
        if side == 0:
            leaving_copy(number).start()
            leaving_copy(number + 1).start()

    def place_halves(number, rows_list, part_of):
        job = jobs[number]
        space = open_space(number)
        for rows in rows_list:
            value = part_of(rows).astype(LOW)
            left, right = value[:, :half], value[:, half:]
            inside = pl.ds(job.lift + rows.start, rows.stop - rows.start)
            space[rows, :] = jnp.where(core == 0, right, left)
            partial[job.slot, inside, :] = jnp.where(core == 0, left, right)
        leaving_copy(number).start()

    total_load.wait()
    grad_ffn = narrow.at[1]
    grad_ffn[...] = grad_total[...].astype(LOW)
    slope_loads = []
    for number in range(4):
        side, chunk = number % 2, number // 2
        active_loads[number].wait()
        space = hidden.at[number // 2, number % 2]
        place_hidden(side, 2 * chunk, lambda rows: dot_columns(space[:, rows], grad_ffn[...]))
        slope_loads.append(load_hidden(slope, number, number))
        if side == 1:
            run_tasks(("out", chunk))

    first_load.wait()
    first_turned = turned.at[0]
    first_turned[...] = narrow[0].T
    token_loads = [mover.start(tokens, narrow.at[0])]
    for number in range(4):
        side, chunk = number % 2, number // 2
        for copy in weight_loads[number]:
            copy.wait()
        slope_loads[number].wait()
        space = hidden.at[number // 2, number % 2]
        part = dot_rows(grad_ffn[...], weights_in[2 + number % 2])
        space[...] = (part * space[...].astype(F32)).astype(LOW)
        place_hidden(side, 4 + 2 * chunk, lambda rows: dot(first_turned[rows, :], space[...]))
        grad_total[...] += dot_rows(space[...], weights_in[number % 2])
        if number + 2 < 4:
            weight_loads.append(load_weights(number + 2))
        run_tasks(("in", number))

    token_loads.append(mover.start(pos_rows, narrow.at[1]))
    output_load = mover.start(output_weight, weights_in.at[0])
    late_loads = [
        mover.start(item, weights_in.at[1 + place])
        for place, item in enumerate((query_weight, key_weight, value_weight))
    ]

    def prob_load(pair, slot):
        return pltpu.make_async_copy(
            prob.at[pl.ds(2 * pair, 2)],
            hidden.at[slot, :, :, pl.ds(0, length)],
            prob_sems.at[slot],
        )

    prob_load(0, 0).start()

    for copy in norm_loads:
        copy.wait()
    vector_load.wait()
    grad_first = grad_total[...]
    vector_steps[0, 2:3, :] = jnp.sum(grad_first * normed_in[...], axis=0, keepdims=True)
    vector_steps[0, 3:4, :] = jnp.sum(grad_first, axis=0, keepdims=True)
    grad_total[...] = norm_backward(grad_first, normed_in[...], scale_in[...], as_row(first_gain))
    narrow[3] = grad_total[...].astype(LOW)
    output_load.wait()
    heads_in[3] = dot_rows(narrow[3], weights_in[0]).astype(LOW)
    run_tasks(("norm", 0))

    context_load.wait()
    context_turned = turned.at[1]
    context_turned[...] = narrow[2].T

    place_halves(8, lower, lambda rows: dot(context_turned[rows, :], narrow[3]))
    run_tasks(("context", 0))

    for copy in head_loads:
        copy.wait()
    flip = flip_matrix()
    matrix[...] = spread_matrix(spread, table)
    (
        query_turned,
        grad_turned,
        query_flip_turned,
        key_flip_turned,
        key_turned,
        tokens_turned,
        pos_turned,
    ) = (turned.at[place] for place in range(7))
    for copy in token_loads:
        copy.wait()
    tokens_turned[...] = narrow[0].T
    pos_turned[...] = narrow[1].T
    grads = narrow
    query_in, key_in, value_in, grad_in = (heads_in.at[place] for place in range(4))
    query_turned[...] = query_in[...].T
    key_turned[...] = key_in[...].T
    grad_turned[...] = grad_in[...].T
    blocks = [slice(at * LANES, (at + 1) * LANES) for at in range(length // LANES)]
    for rows in blocks:
        query_flip_turned[:, rows] = dot(flip, query_in[rows, :]).astype(LOW).T
        key_flip_turned[:, rows] = dot(flip, key_in[rows, :]).astype(LOW).T
    run_tasks(("prepare", 0))

    spans = [slice(side * HEAD_DIM, (side + 1) * HEAD_DIM) for side in range(2)]

    def unskew_pair(pair, straight_turned, flip_turned, table_in, scores_of, turned_sum, table_sum):
        columns = pair_columns(pair)
        head_rows = [
            pl.ds(pl.multiple_of(pair * LANES + side * HEAD_DIM, HEAD_DIM), HEAD_DIM)
            for side in range(2)
        ]
        table_sum[...] = jnp.zeros_like(table_sum)
        straight = [None, None]
        flips = []
        for rows in blocks:
            start = length - rows.stop
            window = slice(start, start + length + LANES)
            moved = []
            for side in range(2):
                left = jnp.concatenate([flip, straight_turned[head_rows[side], rows]], axis=0)
                mixed = scores_of(left, side, rows)
                part = mixed[LANES:]
                straight[side] = part if straight[side] is None else straight[side] + part
                moved.append(unskewed(mixed[:LANES]).astype(LOW))
            for side in range(2):
                table_sum[spans[side], window] += dot(
                    flip_turned[head_rows[side], rows], moved[side]
                )
            stacked = dot(jnp.concatenate(moved, axis=0), table_in[window, columns])
            flips.append(join_heads(stacked))
        for side in range(2):
            turned_sum[spans[side], :] = straight[side]
        return flips

    def pair_tasks(pair, phase):
        for place in range(width // LANES):
            name = ("head", 3 * place + phase)
            if name in TASKS_AFTER:

                @pl.when(pair == place)
                def _():
                    run_tasks(name)

    def send_third(third):
        number = TABLE_JOBS - THIRDS + third
        wide = 2 * LANES
        columns = pl.ds(pl.multiple_of(third * wide, wide), wide)
        job = Job(number, width, 0, number, 0, True)
        before = Job(number - LEAVING, width, 0, number - LEAVING, 0, True)
        space = leaving.at[lax.rem(number, LEAVING)]
        exchange.twin_copy(before, space).wait_send()
        query_grad = dot(tokens_turned[...], grads[0, :, columns])
        query_grad = query_grad + dot_rows(pos_turned[...], grad_pos_queries[columns, :])
        key_grad = dot(tokens_turned[...], grads[1, :, columns])
        key_grad = key_grad + dot_rows(pos_turned[...], grad_pos_keys[columns, :])
        value_grad = dot(tokens_turned[...], grads[2, :, columns])
        for place, value in enumerate((query_grad * factor, key_grad, value_grad)):
            lanes = slice(place * LANES, (place + 1) * LANES)
            low, high = value[:, :LANES].astype(LOW), value[:, LANES:].astype(LOW)
            space[:, lanes] = jnp.where(core == 0, high, low)
            partial[number, :, lanes] = jnp.where(core == 0, low, high)
        exchange.twin_copy(job, space).start()

    def pair_back(pair, carry):
        slot = lax.rem(pair, 2)
        columns = pair_columns(pair)
        pair_rows = pl.ds(pl.multiple_of(pair * LANES, LANES), LANES)
        prob_load(pair, slot).wait()

        @pl.when(pair + 1 < width // LANES)
        def _():
            prob_load(pair + 1, 1 - slot).start()

        value_pair = value_in[:, columns]
        for rows in blocks:
            grad_probs = dot_rows(both_heads(grad_in[rows, columns]), value_pair)
            for side in range(2):
                weights = hidden[slot, side, rows, 0:length].astype(F32)
                product = grad_probs[side * LANES : (side + 1) * LANES] * weights
                shared = jnp.sum(product, axis=-1, keepdims=True)
                grad_scores[side, rows, :] = (product - weights * shared).astype(LOW)
        for side in range(2):
            head_rows = pl.ds(
                pl.multiple_of(pair * LANES + side * HEAD_DIM, HEAD_DIM), HEAD_DIM
            )
            value_turned_sum[spans[side], :] = dot(
                grad_turned[head_rows, :], hidden[slot, side, :, 0:length]
            )
        grads[2, :, columns] = value_turned_sum[...].astype(LOW).T
        pair_tasks(pair, 0)
        flips = unskew_pair(
            pair,
            query_turned,
            query_flip_turned,
            tables_in.at[0],
            lambda left, side, rows: dot(left, grad_scores[side, rows, :]),
            key_turned_sum,
            table_sum,
        )
        for rows, part in zip(blocks, flips):
            flip_sums[rows, :] = split_flip(flip, part)
        summed = dot_rows(table_sum[...].astype(LOW), matrix[...])
        grad_pos_keys[pair_rows, :] = summed.astype(LOW)
        pair_tasks(pair, 1)
        flips = unskew_pair(
            pair,
            key_turned,
            key_flip_turned,
            tables_in.at[1],
            lambda left, side, rows: dot_rows(left, grad_scores[side, :, rows]),
            query_turned_sum,
            table_sum,
        )
        for rows, part in zip(blocks, flips):
            summed = key_turned_sum[:, rows].T + split_flip(flip, part)
            grads[1, rows, columns] = summed.astype(LOW)
            summed = query_turned_sum[:, rows].T + flip_sums[rows, :]
            grads[0, rows, columns] = summed.astype(LOW)
        summed = dot_rows(table_sum[...].astype(LOW), matrix[...])
        grad_pos_queries[pair_rows, :] = summed.astype(LOW)

        @pl.when(lax.rem(pair, 2) == 1)
        def _():
            send_third(pair // 2)

        pair_tasks(pair, 2)
        return carry

    lax.fori_loop(0, width // LANES, pair_back, 0)

    for copy in late_loads:
        copy.wait()

    for part in range(2):
        shift = part * table // 2
        rows = slice(0, table // 2)

        def table_part(rows):
            inside = slice(shift + rows.start, shift + rows.stop)
            turned_dims = (((0,), (1,)), ((), ()))
            summed = lax.dot_general(
                grad_pos_keys[:, inside], weights_in[2], turned_dims, preferred_element_type=F32
            )
            return summed + factor * lax.dot_general(
                grad_pos_queries[:, inside], weights_in[1], turned_dims, preferred_element_type=F32
            )

        place_halves(TABLE_JOBS + part, [rows], table_part)
    run_tasks(("table", 0))
    tokens_grad_low = narrow.at[3]
    for rows in blocks:
        summed = grad_total[rows, :] + factor * dot_rows(grads[0, rows, :], weights_in[1])
        summed = summed + dot_rows(grads[1, rows, :], weights_in[2])
        summed = summed + dot_rows(grads[2, rows, :], weights_in[3])
        tokens_grad_low[rows, :] = summed.astype(LOW)
    mover.leave(tokens_grad_low, tokens_grad)
    run_tasks(("tail", 0))
    exchange.finish()
    for number in range(JOB_COUNT - LEAVING, JOB_COUNT):
        leaving_copy(number).wait_send()
    for step in range(len(vector_partners)):
        vector_copy(step).wait_send()
    mover.finish()


def gradients(
    activation,
    slope,
    in_weights,
    out_weights,
    first_low,
    grad_pre2,
    normed1,
    scale1,
    first_gain,
    output_weight,
    vectors,
    context,
    prob,
    query,
    key,
    value,
    key_table,
    query_table,
    tokens,
    pos_rows,
    query_weight,
    key_weight,
    value_weight,
):
    length, width = tokens.shape
    table = pos_rows.shape[0]
    half = width // 2
    inputs = (
        activation,
        slope,
        in_weights,
        out_weights,
        first_low,
        grad_pre2,
        normed1,
        scale1,
        first_gain,
        output_weight,
        vectors,
        context,
        prob,
        query,
        key,
        value,
        key_table,
        query_table,
        tokens,
        pos_rows,
        query_weight,
        key_weight,
        value_weight,
        jnp.asarray(spread_index(length)),
    )
    anywhere = pl.BlockSpec(memory_space=pl.ANY)
    local = pl.BlockSpec(memory_space=pltpu.VMEM)
    outs = [
        jax.ShapeDtypeStruct((width, 2 * width), LOW),
        jax.ShapeDtypeStruct((2 * width, width), LOW),
        jax.ShapeDtypeStruct((2 * THIRDS, width, half), LOW),
        jax.ShapeDtypeStruct((width, width), LOW),
        jax.ShapeDtypeStruct((table, width), LOW),
        jax.ShapeDtypeStruct((length, width), LOW),
        jax.ShapeDtypeStruct(vectors.shape, F32),
    ]
    slots = TABLE_JOBS + 1
    scratch = [
        pltpu.VMEM((slots, width, half), LOW),
        pltpu.VMEM((slots, width, half), LOW),
        pltpu.VMEM((slots, width // 16 * 15, half), LOW),
        pltpu.VMEM((LEAVING, width, half), LOW),
        pltpu.VMEM((2, 2, length, width), LOW),
        pltpu.VMEM((4, length, width), LOW),
        pltpu.VMEM((4, length, width), LOW),
        pltpu.VMEM((2, 2 * length, width), LOW),
        pltpu.VMEM((4, width, width), LOW),
        pltpu.VMEM((7, width, length), LOW),
        pltpu.VMEM((2, length, length), LOW),
        pltpu.VMEM((length, LANES), F32),
        pltpu.VMEM((LANES, length), F32),
        pltpu.VMEM((LANES, length), F32),
        pltpu.VMEM((LANES, length), F32),
        pltpu.VMEM((LANES, 2 * length), F32),
        pltpu.VMEM((table, 2 * length), LOW),
        pltpu.VMEM((width, table), LOW),
        pltpu.VMEM((width, table), LOW),
        pltpu.VMEM((length, width), F32),
        pltpu.VMEM((length, width), F32),
        pltpu.VMEM((length, 1), F32),
        pltpu.VMEM((2 + PAIR_BITS,) + vectors.shape, F32),
        pltpu.VMEM((1 + PAIR_BITS,) + vectors.shape, F32),
        pltpu.SemaphoreType.DMA((JOB_COUNT, 11)),
        pltpu.SemaphoreType.DMA((JOB_COUNT, 10)),
        pltpu.SemaphoreType.DMA((1 + PAIR_BITS,)),
        pltpu.SemaphoreType.DMA((1 + PAIR_BITS,)),
        pltpu.SemaphoreType.DMA((2,)),
        pltpu.SemaphoreType.DMA((64,)),
    ]
    return pl.pallas_call(
        gradient_kernel,
        in_specs=[local if at in (8, 23) else anywhere for at in range(len(inputs))],
        out_specs=[anywhere] * (len(outs) - 1) + [local],
        out_shape=outs,
        scratch_shapes=scratch,
        compiler_params=pltpu.CompilerParams(
            vmem_limit_bytes=GRADIENT_VMEM_BYTES, collective_id=0, has_side_effects=True
        ),
        name="gradients",
    )(*inputs)


def finish_kernel(
    in_share,
    out_share,
    output_share,
    heads_share,
    table_share,
    position_table,
    output_in,
    tokens_in,
    vectors,
    table_gain,
    in_grad,
    out_grad,
    output_grad,
    query_grad,
    key_grad,
    value_grad,
    table_grad,
    output,
    tokens_grad,
    gain_grad,
    shift_grad,
    *rest,
):
    vector_grads, rest = rest[:4], rest[4:]
    in_low, in_wide, out_low, out_wide, output_low, output_wide, heads_low, *rest = rest
    query_wide, key_wide, value_wide, table_low, table_wide, position_in, *rest = rest
    output_space, tokens_space, sems = rest
    mover = Mover(sems)
    width = output_share.shape[0]
    half = width // 2

    def cuts(source, low, wide, target):
        pieces = []
        for start in range(0, source.shape[0], half):
            rows = pl.ds(start, half)
            pieces.append(
                (mover.start(source.at[rows], low.at[rows]), low, wide, target, rows)
            )
        return pieces

    pieces = cuts(in_share, in_low, in_wide, in_grad)
    pieces += cuts(out_share, out_low, out_wide, out_grad)
    pieces += cuts(output_share, output_low, output_wide, output_grad)
    head_loads = [
        mover.start(heads_share.at[:, pl.ds(start, half)], heads_low.at[:, pl.ds(start, half)])
        for start in range(0, width, half)
    ]
    table_load = mover.start(table_share, table_low)
    position_load = mover.start(position_table, position_in)
    passing = [
        (mover.start(source, space), space, target)
        for source, space, target in (
            (output_in, output_space, output),
            (tokens_in, tokens_space, tokens_grad),
        )
    ]
    for load, low, wide, target, rows in pieces:
        load.wait()
        wide[rows, :] = low[rows, :].astype(F32)
        mover.leave(wide.at[rows], target.at[rows])
    for number, load in enumerate(head_loads):
        load.wait()
        rows = slice(number * half, (number + 1) * half)
        for place, (wide, target) in enumerate(
            ((query_wide, query_grad), (key_wide, key_grad), (value_wide, value_grad))
        ):
            for block in range(2 * THIRDS):
                lanes = slice(place * LANES, (place + 1) * LANES)
                columns = slice(block * LANES, (block + 1) * LANES)
                wide[rows, columns] = heads_low[block, rows, lanes].astype(F32)
            mover.leave(wide.at[rows], target.at[rows])
    for load, space, target in passing:
        load.wait()
        mover.leave(space, target)
    table_load.wait()
    position_load.wait()
    gain = as_row(table_gain)
    grad = table_low[...].astype(F32)
    _, normed, scale_rows = norm_forward(position_in[...].astype(F32), gain, 0.0)
    table_wide[...] = norm_backward(grad, normed, scale_rows, gain)
    mover.leave(table_wide, table_grad)
    gain_grad[...] = jnp.sum(grad * normed, axis=0)
    shift_grad[...] = jnp.sum(grad, axis=0)
    for place, target in enumerate(vector_grads):
        target[...] = vectors[place, :]
    mover.finish()


def finish(shares, vectors, position_table, table_gain, output, tokens_grad):
    in_share, out_share, heads_share, output_share, table_share = shares
    table, width = position_table.shape
    inputs = (
        in_share,
        out_share,
        output_share,
        heads_share,
        table_share,
        position_table,
        output,
        tokens_grad,
        vectors,
        table_gain,
    )
    anywhere = pl.BlockSpec(memory_space=pl.ANY)
    local = pl.BlockSpec(memory_space=pltpu.VMEM)

    def wide(item):
        return jax.ShapeDtypeStruct(item.shape, F32)

    square = jax.ShapeDtypeStruct((width, width), F32)
    vector = jax.ShapeDtypeStruct((width,), F32)
    outs = [wide(in_share), wide(out_share), square, square, square, square, wide(table_share)]
    outs += [jax.ShapeDtypeStruct(item.shape, LOW) for item in (output, tokens_grad)]
    outs += [vector] * 6
    scratch = []
    for item in (in_share, out_share, output_share):
        scratch += [pltpu.VMEM(item.shape, LOW), pltpu.VMEM(item.shape, F32)]
    scratch += [pltpu.VMEM(heads_share.shape, LOW)] + [pltpu.VMEM((width, width), F32)] * 3
    scratch += [pltpu.VMEM((table, width), LOW), pltpu.VMEM((table, width), F32)]
    scratch += [pltpu.VMEM(item.shape, LOW) for item in (position_table, output, tokens_grad)]
    scratch.append(pltpu.SemaphoreType.DMA((64,)))
    return pl.pallas_call(
        finish_kernel,
        in_specs=[anywhere] * 8 + [local] * 2,
        out_specs=[anywhere] * 9 + [local] * 6,
        out_shape=outs,
        scratch_shapes=scratch,
        compiler_params=pltpu.CompilerParams(vmem_limit_bytes=VMEM_BYTES),
        name="finish",
    )(*inputs)


def beyond(shares):
    in_share, out_share, *others = shares
    chips = 1 << PAIR_BITS
    rows, columns = lax.axis_size("rows"), lax.axis_size("cols")
    if rows > chips:
        groups = [[at + chips * step for step in range(rows // chips)] for at in range(chips)]
        in_share, out_share, *others = lax.psum(
            (in_share, out_share, *others), "rows", axis_index_groups=groups
        )
    if columns > 2:
        groups = [[at + 2 * step for step in range(columns // 2)] for at in range(2)]
        others = lax.psum(tuple(others), "cols", axis_index_groups=groups)
        in_share = lax.psum_scatter(
            in_share, "cols", scatter_dimension=1, axis_index_groups=groups, tiled=True
        )
        out_share = lax.psum_scatter(
            out_share, "cols", scatter_dimension=0, axis_index_groups=groups, tiled=True
        )
    return (in_share, out_share, *others)


def on_device(
    tokens,
    segment_ids,
    position_table,
    table_gain,
    table_shift,
    query_weight,
    key_weight,
    value_weight,
    output_weight,
    first_gain,
    first_shift,
    feedforward_input_weight,
    ffn_out,
    second_gain,
    second_shift,
    out_grad,
):
    (
        query,
        key,
        value,
        prob,
        context,
        normed1,
        scale1,
        first_low,
        key_table,
        query_table,
        pos_rows,
        in_weights,
        out_weights,
        activation,
        slope,
        grad_pre2,
        output,
        vectors,
    ) = forward(
        tokens,
        segment_ids,
        position_table,
        table_gain,
        table_shift,
        query_weight,
        key_weight,
        value_weight,
        output_weight,
        first_gain,
        first_shift,
        feedforward_input_weight,
        ffn_out,
        second_gain,
        second_shift,
        out_grad,
    )
    shares = gradients(
        activation,
        slope,
        in_weights,
        out_weights,
        first_low,
        grad_pre2,
        normed1,
        scale1,
        first_gain,
        output_weight,
        vectors,
        context,
        prob,
        query,
        key,
        value,
        key_table,
        query_table,
        tokens,
        pos_rows,
        query_weight,
        key_weight,
        value_weight,
    )
    *sums, vectors = beyond(shares[:5] + shares[6:])
    (
        in_grad,
        out_weight_grad,
        output_weight_grad,
        query_grad,
        key_grad,
        value_grad,
        table_grad,
        output,
        tokens_grad,
        table_gain_grad,
        table_shift_grad,
        second_gain_grad,
        second_shift_grad,
        first_gain_grad,
        first_shift_grad,
    ) = finish(sums, vectors, position_table, table_gain, output, shares[5])
    return (
        output,
        tokens_grad,
        table_grad,
        table_gain_grad,
        table_shift_grad,
        query_grad,
        key_grad,
        value_grad,
        output_weight_grad,
        first_gain_grad,
        first_shift_grad,
        in_grad,
        out_weight_grad,
        second_gain_grad,
        second_shift_grad,
    )


def solution(mesh):
    spread = P(("rows", "cols"), None)
    in_specs = (spread, spread) + (P(),) * 9 + (P(None, "cols"), P("cols", None), P(), P(), spread)
    out_specs = (
        (spread, spread) + (P(),) * 9 + (P(None, "cols"), P("cols", None), P(), P())
    )
    return jax.shard_map(
        on_device, mesh=mesh, in_specs=in_specs, out_specs=out_specs, check_vma=False
    )
```

```python
import math

import jax
import jax.numpy as jnp
import numpy as np
from jax import lax
from jax.experimental import pallas as pl
from jax.experimental.pallas import tpu as pltpu
from jax.sharding import PartitionSpec as P

HEAD_DIM = 64
BUCKETS = 256
MAX_POS = 512
EPSILON = 1e-07
NEGATIVE = -1e30
ROOT_HALF = 0.7071067811865476
DENSITY_SCALE = 0.3989422804014327
LOG2_E = 1.4426950408889634

LANES = 128
VMEM_BYTES = 56 * 1024 * 1024
GRADIENT_VMEM_BYTES = 60 * 1024 * 1024
F32 = jnp.float32
LOW = jnp.bfloat16


def bucket_table(length):
    middle = BUCKETS // 2
    distance = np.arange(-(length - 1), length)
    direction = np.sign(distance)
    magnitude = np.where((distance < middle) & (distance > -middle), middle - 1, np.abs(distance))
    logged = (
        np.ceil(np.log(magnitude / middle) / np.log((MAX_POS - 1) / middle) * (middle - 1)) + middle
    )
    bucket = np.where(magnitude <= middle, distance, logged * direction)
    return np.clip(bucket + BUCKETS, 0, 2 * BUCKETS - 1).astype(np.int32)


def spread_index(length):
    table = np.concatenate([bucket_table(length)[::-1], [-1]]).astype(np.int32)
    return table.reshape(1, 2 * length)


def dot(left, right):
    return jnp.dot(left, right, preferred_element_type=F32)


def dot_rows(left, right):
    return lax.dot_general(left, right, (((1,), (1,)), ((), ())), preferred_element_type=F32)


def dot_columns(left, right):
    return lax.dot_general(left, right, (((0,), (0,)), ((), ())), preferred_element_type=F32)


def norm_forward(value, gain, shift):
    centered = value - jnp.mean(value, axis=-1, keepdims=True)
    squared_spread = jnp.mean(centered * centered, axis=-1, keepdims=True)
    scale_rows = lax.rsqrt(squared_spread + EPSILON)
    normed = centered * scale_rows
    return (normed * gain + shift, normed, scale_rows)


def norm_backward(grad, normed, scale_rows, gain):
    scaled = grad * gain
    return scale_rows * (
        scaled
        - jnp.mean(scaled, axis=-1, keepdims=True)
        - normed * jnp.mean(scaled * normed, axis=-1, keepdims=True)
    )


def pair_columns(pair):
    return pl.ds(pl.multiple_of(pair * LANES, LANES), LANES)


def head_lanes(rows, half):
    lane = lax.broadcasted_iota(jnp.int32, (rows, LANES), 1)
    return (lane < HEAD_DIM) if half == 0 else (lane >= HEAD_DIM)


def spread_columns(index_ref, buckets):
    column = lax.broadcasted_iota(jnp.int32, (index_ref.shape[0], buckets), 1)
    return jnp.where(index_ref[...] == column, 1.0, 0.0).astype(LOW)


def spread_matrix(index_ref, buckets):
    row = lax.broadcasted_iota(jnp.int32, (buckets, index_ref.shape[1]), 0)
    return jnp.where(index_ref[...] == row, 1.0, 0.0).astype(LOW)


def flip_matrix():
    row = lax.broadcasted_iota(jnp.int32, (LANES, LANES), 0)
    column = lax.broadcasted_iota(jnp.int32, (LANES, LANES), 1)
    return jnp.where(row + column == LANES - 1, 1.0, 0.0).astype(LOW)


def unit_matrix():
    row = lax.broadcasted_iota(jnp.int32, (LANES, LANES), 0)
    column = lax.broadcasted_iota(jnp.int32, (LANES, LANES), 1)
    return jnp.where(row == column, 1.0, 0.0).astype(LOW)


def both_heads(pair_rows):
    rows = pair_rows.shape[0]
    return jnp.concatenate(
        [jnp.where(head_lanes(rows, half), pair_rows, 0) for half in range(2)], axis=0
    )


def join_heads(stacked):
    rows = stacked.shape[0] // 2
    return jnp.where(head_lanes(rows, 0), stacked[:rows], stacked[rows:])


def tiles_of(value):
    return [value[:, at : at + LANES] for at in range(0, value.shape[1], LANES)]


def turn(tile, first):
    return pltpu.roll(tile, first, 1, stride=1, stride_axis=0)


def lane_from(distance):
    row = lax.broadcasted_iota(jnp.int32, (LANES, LANES), 0)
    lane = lax.broadcasted_iota(jnp.int32, (LANES, LANES), 1)
    return lane >= row + distance


def skewed(window, length):
    turned = [turn(tile, 1) for tile in tiles_of(window)]
    late = lane_from(1)
    parts = [jnp.where(late, after, tile) for tile, after in zip(turned, turned[1:])]
    return jnp.concatenate(parts, axis=1)


def unskewed(flipped):
    turned = [turn(tile, 0) for tile in tiles_of(flipped)]
    late = lane_from(0)
    nothing = jnp.zeros_like(turned[0])
    before, after = [nothing] + turned, turned + [nothing]
    parts = [jnp.where(late, tile, left) for left, tile in zip(before, after)]
    return jnp.concatenate(parts, axis=1)


def as_row(vector):
    return vector[...].reshape(1, vector.shape[0])


def whole(shape):
    zeros = (0,) * len(shape)
    return pl.BlockSpec(shape, lambda *_: zeros, pipeline_mode=pl.Buffered(1))


def whole_out(shape):
    zeros = (0,) * len(shape)
    return pl.BlockSpec(shape, lambda *_: zeros)


def gelu_parts(value):
    divisor = 1.0 + (0.3275911 * ROOT_HALF) * jnp.abs(value)
    guess = pl.reciprocal(divisor, approx=True)
    part = guess * (2.0 - divisor * guess)
    part = part * (2.0 - divisor * part)
    bell = jnp.exp2((-0.5 * LOG2_E) * (value * value))
    series = (0.5 * 1.061405429) * part - (0.5 * 1.453152027)
    series = series * part + (0.5 * 1.421413741)
    series = series * part - (0.5 * 0.284496736)
    series = series * part + (0.5 * 0.254829592)
    tail = series * (part * bell)
    return jnp.where(value < 0.0, tail, 1.0 - tail), (DENSITY_SCALE * value) * bell


class Mover:
    def __init__(self, sems):
        self.sems, self.count, self.open = sems, 0, []

    def start(self, source, target):
        copy = pltpu.make_async_copy(source, target, self.sems.at[self.count])
        self.count += 1
        copy.start()
        return copy

    def leave(self, source, target):
        self.open.append(self.start(source, target))

    def finish(self):
        for copy in self.open:
            copy.wait()


def unit_order(parts):
    return [(place % (parts // 2)) * 2 + place // (parts // 2) for place in range(parts)]


def forward_kernel(
    tokens,
    segments,
    table,
    table_gain,
    table_shift,
    query_weight,
    key_weight,
    value_weight,
    output_weight,
    first_gain,
    first_shift,
    in_weight,
    out_weight,
    second_gain,
    second_shift,
    out_grad,
    spread,
    query_out,
    key_out,
    value_out,
    prob_out,
    context_out,
    normed_out,
    scale_out,
    first_low_out,
    key_table_out,
    query_table_out,
    pos_rows_out,
    in_weights_out,
    out_weights_out,
    activation_out,
    slope_out,
    grad_pre2_out,
    output_out,
    vectors_out,
    tokens_in,
    table_in,
    weights_in,
    out_grad_in,
    heads_in,
    tables_in,
    pos_rows_in,
    probs,
    context,
    normed,
    scale,
    first_low,
    total,
    in_weights,
    out_weights,
    inner,
    activation,
    slope,
    output,
    vectors,
    mask,
    crossed,
    send_sems,
    receive_sems,
    prob_sems,
    move_sems,
):
    length, width = tokens.shape
    parts, _, units = in_weights.shape
    factor = 1.0 / math.sqrt(3 * HEAD_DIM)
    row, me = lax.axis_index("rows"), lax.axis_index("cols")
    mover = Mover(move_sems)
    table_load = mover.start(table, table_in)
    key_load = mover.start(key_weight, weights_in.at[1])
    query_load = mover.start(query_weight, weights_in.at[0])
    tokens_load = mover.start(tokens, tokens_in)
    value_load = mover.start(value_weight, weights_in.at[2])
    output_load = mover.start(output_weight, weights_in.at[3])
    grad_load = mover.start(out_grad, out_grad_in)
    own_loads = [
        mover.start(in_weight, in_weights.at[me]),
        mover.start(out_weight, out_weights.at[me]),
    ]
    peers = [lax.rem(me + step, parts) for step in range(1, parts)]
    barrier = pltpu.get_barrier_semaphore()
    for peer in peers:
        pl.semaphore_signal(
            barrier, inc=1, device_id=(row, peer), device_id_type=pl.DeviceIdType.MESH
        )
    pl.semaphore_wait(barrier, parts - 1)

    def shard_copy(kind, step, place):
        source, target = ((in_weight, in_weights), (out_weight, out_weights))[kind]
        return pltpu.make_async_remote_copy(
            src_ref=source,
            dst_ref=target.at[place],
            send_sem=send_sems.at[kind, step],
            recv_sem=receive_sems.at[kind, step],
            device_id=(row, peers[step]),
            device_id_type=pl.DeviceIdType.MESH,
        )

    for kind in range(2):
        for step in range(parts - 1):
            shard_copy(kind, step, me).start()

    key_load.wait()
    query_load.wait()
    table_load.wait()
    pos_out, _, _ = norm_forward(table_in[...].astype(F32), as_row(table_gain), as_row(table_shift))
    pos_rows_in[...] = pos_out.astype(LOW)
    mover.leave(pos_rows_in, pos_rows_out)
    matrix = spread_columns(spread, table.shape[0])
    pos_keys = dot(pos_rows_in[...], weights_in[1]).astype(LOW)
    tables_in[0] = dot(matrix, pos_keys).astype(LOW)
    pos_queries = (dot(pos_rows_in[...], weights_in[0]) * factor).astype(LOW)
    tables_in[1] = dot(matrix, pos_queries).astype(LOW)
    mover.leave(tables_in.at[0], key_table_out)
    mover.leave(tables_in.at[1], query_table_out)
    tokens_load.wait()
    heads_in[0] = (dot(tokens_in[...], weights_in[0]) * factor).astype(LOW)
    heads_in[1] = dot(tokens_in[...], weights_in[1]).astype(LOW)
    value_load.wait()
    heads_in[2] = dot(tokens_in[...], weights_in[2]).astype(LOW)
    for place, target in enumerate((query_out, key_out, value_out)):
        mover.leave(heads_in.at[place], target)
    document = lax.broadcasted_iota(jnp.int32, (8, length), 0)
    member = jnp.where(segments[...] == document, 1.0, 0.0).astype(LOW)
    mask[...] = jnp.where(dot_columns(member, member) > 0.5, 0.0, NEGATIVE)

    blocks = [slice(at * LANES, (at + 1) * LANES) for at in range(length // LANES)]
    unit = unit_matrix()

    pairs = width // LANES

    def prob_copy(pair):
        heads = pl.ds(2 * pair, 2)
        return pltpu.make_async_copy(probs.at[heads], prob_out.at[heads], prob_sems.at[pair])

    def one_pair(pair, carry):
        columns = pair_columns(pair)
        query_pair = heads_in[0, :, columns]
        key_pair = heads_in[1, :, columns]
        value_pair = heads_in[2, :, columns]
        for rows in blocks:
            start = length - rows.stop
            keys = both_heads(key_pair[rows])
            window = dot_rows(keys, tables_in[1, start : start + length + LANES, columns])
            for half in range(2):
                part = window[half * LANES : (half + 1) * LANES]
                crossed[half, rows, :] = skewed(part, length).astype(LOW)
        for rows in blocks:
            start = length - rows.stop
            queries = both_heads(query_pair[rows])
            window = dot_rows(queries, tables_in[0, start : start + length + LANES, columns])
            for half in range(2):
                span = slice(half * LANES, (half + 1) * LANES)
                left = jnp.concatenate([queries[span], unit], axis=1)
                right = jnp.concatenate([key_pair, crossed[half, :, rows]], axis=1)
                scores = dot_rows(left, right) + skewed(window[span], length) + mask[rows, :]
                top = jnp.max(scores, axis=-1, keepdims=True)
                weights = jnp.exp(scores - top)
                share = jnp.sum(weights, axis=-1, keepdims=True)
                probs[2 * pair + half, rows, :] = (weights * (1.0 / share)).astype(LOW)
        contexts = [dot(probs[2 * pair + half], value_pair) for half in range(2)]
        joined = jnp.where(head_lanes(length, 0), contexts[0], contexts[1])
        context[:, columns] = joined.astype(LOW)
        prob_copy(pair).start()
        return carry

    lax.fori_loop(0, pairs, one_pair, 0)
    mover.leave(context, context_out)

    output_load.wait()
    halves = [slice(at, at + length // 2) for at in range(0, length, length // 2)]
    for rows in halves:
        pre = dot(context[rows, :], weights_in[3]) + tokens_in[rows, :].astype(F32)
        first, first_normed, scale_rows = norm_forward(pre, as_row(first_gain), as_row(first_shift))
        total[rows, :] = first
        first_low[rows, :] = first.astype(LOW)
        normed[rows, :] = first_normed
        scale[rows, :] = scale_rows
    mover.leave(first_low, first_low_out)
    mover.leave(normed, normed_out)
    mover.leave(scale, scale_out)

    for copy in own_loads:
        copy.wait()
    for kind in range(2):
        for step in range(parts - 1):
            shard_copy(kind, step, lax.rem(me + parts - 1 - step, parts)).wait_recv()
    mover.leave(in_weights, in_weights_out)
    mover.leave(out_weights, out_weights_out)
    size = math.gcd(units, width)
    chunks = [
        (part, slice(at, at + size)) for part in unit_order(parts) for at in range(0, units, size)
    ]

    def begin(number, rows):
        part, cut = chunks[number]
        inner[number % 2, rows, :] = dot(first_low[rows, :], in_weights[part, :, cut])

    for rows in halves:
        begin(0, rows)
    for number, (part, cut) in enumerate(chunks):
        columns = slice(number * size, (number + 1) * size)
        for rows in halves:
            if number + 1 < len(chunks):
                begin(number + 1, rows)
            value = inner[number % 2, rows, :]
            cumulative, bent = gelu_parts(value)
            activation[rows, columns] = (value * cumulative).astype(LOW)
            slope[rows, columns] = (cumulative + bent).astype(LOW)
            total[rows, :] += dot(activation[rows, columns], out_weights[part, cut, :])
        mover.leave(activation.at[:, columns], activation_out.at[:, columns])
        mover.leave(slope.at[:, columns], slope_out.at[:, columns])
    grad_load.wait()
    gain_sum = jnp.zeros((1, width), F32)
    shift_sum = jnp.zeros((1, width), F32)
    for rows in halves:
        second, second_normed, scale_rows = norm_forward(
            total[rows, :], as_row(second_gain), as_row(second_shift)
        )
        output[rows, :] = second.astype(LOW)
        grad_out = out_grad_in[rows, :].astype(F32)
        gain_sum = gain_sum + jnp.sum(grad_out * second_normed, axis=0, keepdims=True)
        shift_sum = shift_sum + jnp.sum(grad_out, axis=0, keepdims=True)
        total[rows, :] = norm_backward(grad_out, second_normed, scale_rows, as_row(second_gain))
    mover.leave(total, grad_pre2_out)
    mover.leave(output, output_out)
    vectors[0:1, :] = gain_sum
    vectors[1:2, :] = shift_sum
    vectors[2:8, :] = jnp.zeros((6, width), F32)
    mover.leave(vectors, vectors_out)
    for kind in range(2):
        for step in range(parts - 1):
            shard_copy(kind, step, me).wait_send()
    for pair in range(pairs):
        prob_copy(pair).wait()
    mover.finish()


def forward(
    tokens,
    segment_ids,
    table,
    table_gain,
    table_shift,
    query_weight,
    key_weight,
    value_weight,
    output_weight,
    first_gain,
    first_shift,
    in_weight,
    out_weight,
    second_gain,
    second_shift,
    out_grad,
):
    length, width = tokens.shape
    heads = width // HEAD_DIM
    parts, units = lax.axis_size("cols"), in_weight.shape[1]
    hidden = parts * units
    chunk = math.gcd(units, width)
    inputs = (
        tokens,
        segment_ids,
        table,
        table_gain,
        table_shift,
        query_weight,
        key_weight,
        value_weight,
        output_weight,
        first_gain,
        first_shift,
        in_weight,
        out_weight,
        second_gain,
        second_shift,
        out_grad,
        jnp.asarray(spread_index(length).reshape(2 * length, 1)),
    )
    anywhere = pl.BlockSpec(memory_space=pl.ANY)
    local = pl.BlockSpec(memory_space=pltpu.VMEM)
    in_specs = [local if at in (1, 3, 4, 9, 10, 13, 14, 16) else anywhere for at in range(17)]

    def low(*shape):
        return jax.ShapeDtypeStruct(shape, LOW)

    def wide(*shape):
        return jax.ShapeDtypeStruct(shape, F32)

    outs = [
        low(length, width),
        low(length, width),
        low(length, width),
        low(heads, length, length),
        low(length, width),
        wide(length, width),
        wide(length, 1),
        low(length, width),
        low(2 * length, width),
        low(2 * length, width),
        low(*table.shape),
        low(parts, width, units),
        low(parts, units, width),
        low(length, hidden),
        low(length, hidden),
        wide(length, width),
        low(length, width),
        wide(8, width),
    ]
    scratch = [
        pltpu.VMEM((length, width), LOW),
        pltpu.VMEM(table.shape, LOW),
        pltpu.VMEM((4, width, width), LOW),
        pltpu.VMEM((length, width), LOW),
        pltpu.VMEM((3, length, width), LOW),
        pltpu.VMEM((2, 2 * length, width), LOW),
        pltpu.VMEM(table.shape, LOW),
        pltpu.VMEM((heads, length, length), LOW),
        pltpu.VMEM((length, width), LOW),
        pltpu.VMEM((length, width), F32),
        pltpu.VMEM((length, 1), F32),
        pltpu.VMEM((length, width), LOW),
        pltpu.VMEM((length, width), F32),
        pltpu.VMEM((parts, width, units), LOW),
        pltpu.VMEM((parts, units, width), LOW),
        pltpu.VMEM((2, length, chunk), F32),
        pltpu.VMEM((length, hidden), LOW),
        pltpu.VMEM((length, hidden), LOW),
        pltpu.VMEM((length, width), LOW),
        pltpu.VMEM((8, width), F32),
        pltpu.VMEM((length, length), F32),
        pltpu.VMEM((2, length, length), LOW),
        pltpu.SemaphoreType.DMA((2, parts - 1)),
        pltpu.SemaphoreType.DMA((2, parts - 1)),
        pltpu.SemaphoreType.DMA((heads // 2,)),
        pltpu.SemaphoreType.DMA((24 + 2 * (hidden // chunk),)),
    ]
    return pl.pallas_call(
        forward_kernel,
        in_specs=in_specs,
        out_specs=[anywhere] * len(outs),
        out_shape=outs,
        scratch_shapes=scratch,
        compiler_params=pltpu.CompilerParams(
            vmem_limit_bytes=VMEM_BYTES, collective_id=1, has_side_effects=True
        ),
        name="forward",
    )(*inputs)


def split_flip(matrix, value):
    high = value.astype(LOW)
    rest = (value - high.astype(F32)).astype(LOW)
    return dot(matrix, high) + dot(matrix, rest)


PAIR_BITS = 4
TABLE_JOBS = 12
JOB_COUNT = 14
LEAVING = 3
THIRDS = 3
ORDERS = (
    (0, 2, 1, 3),
    (1, 2, 0, 3),
    (0, 1, 2, 3),
    (1, 0, 2, 3),
    (2, 0, 1, 3),
    (2, 1, 0, 3),
    (0, 2, 3, 1),
    (1, 2, 3, 0),
)
COLOURS = (5, 1, 2, 2, 1, 4, 4, 3, 0, 1, 2, 3, 4, 2)
TASKS_AFTER = {
    ("out", 1): (
        (0, 0), (1, 0),
    ),
    ("in", 0): (
        (2, 0),
    ),
    ("in", 1): (
        (4, 0), (3, 0), (5, 0),
    ),
    ("norm", 0): (
        (0, 1), (1, 1), (14, 0),
    ),
    ("context", 0): (
        (7, 0), (14, 1),
    ),
    ("prepare", 0): (
        (5, 1), (14, 2),
    ),
    ("head", 0): (
        (4, 1), (6, 0),
    ),
    ("head", 1): (
        (8, 0),
    ),
    ("head", 2): (
        (14, 3),
    ),
    ("head", 4): (
        (3, 1), (5, 2), (14, 4),
    ),
    ("head", 6): (
        (4, 2), (14, 5),
    ),
    ("head", 8): (
        (1, 2), (0, 2), (2, 1), (8, 1), (7, 1),
    ),
    ("head", 9): (
        (4, 3), (5, 3), (9, 0), (3, 2),
    ),
    ("head", 12): (
        (4, 4), (2, 2),
    ),
    ("head", 13): (
        (0, 3), (7, 2), (10, 0),
    ),
    ("head", 15): (
        (1, 3), (4, 5),
    ),
    ("head", 16): (
        (9, 1), (8, 2), (3, 3),
    ),
    ("head", 17): (
        (6, 1), (7, 3),
    ),
    ("table", 0): (
        (8, 3), (11, 0), (12, 0), (3, 4), (4, 6), (0, 4), (6, 2), (7, 4), (13, 0), (8, 4),
        (3, 5), (9, 2), (5, 4), (0, 5), (10, 1), (6, 3), (8, 5), (1, 4), (12, 1), (7, 5),
        (5, 5), (11, 1), (9, 3), (12, 2), (3, 6), (6, 4), (13, 1), (10, 2), (5, 6), (9, 4),
        (7, 6), (4, 7), (11, 2), (12, 3), (10, 3), (9, 5), (8, 6), (11, 3), (6, 5), (1, 5),
        (0, 6), (3, 7), (10, 4), (11, 4), (13, 2), (10, 5), (9, 6), (12, 4), (13, 3),
        (7, 7), (2, 3),
    ),
    ("tail", 0): (
        (12, 5), (8, 7), (11, 5), (2, 4), (1, 6), (13, 4), (10, 6), (9, 7), (0, 7), (6, 6),
        (11, 6), (12, 6), (2, 5), (13, 5), (13, 6), (8, 8), (12, 7), (2, 6), (10, 7),
        (11, 7), (13, 7), (6, 7), (2, 7), (9, 8), (7, 8), (12, 8), (8, 9), (1, 7), (5, 7),
        (3, 8), (10, 8), (13, 8), (9, 9), (4, 8), (12, 9), (13, 9), (0, 8), (11, 8), (6, 8),
        (11, 9), (2, 8), (10, 9), (5, 8), (1, 8),
    ),
}


class Job:
    def __init__(self, number, rows, colour, slot, lift, gathered):
        self.number, self.rows, self.colour = number, rows, colour
        self.slot, self.lift, self.gathered = slot, lift, gathered

    def received(self, stage):
        start = sum(self.rows >> (step + 1) for step in range(stage))
        return (self.lift // 16 * 15) + start, self.rows >> (stage + 1)


def make_jobs(height, table):
    jobs = [Job(n, height, COLOURS[n], n, 0, n >= 8) for n in range(TABLE_JOBS)]
    jobs.append(Job(TABLE_JOBS, table // 2, COLOURS[TABLE_JOBS], TABLE_JOBS, 0, True))
    jobs.append(Job(TABLE_JOBS + 1, table // 2, COLOURS[TABLE_JOBS + 1], TABLE_JOBS, table // 2, True))
    return jobs


class Exchange:
    def __init__(self, partial, landed, received, send_sems, receive_sems, outs, jobs):
        self.partial, self.landed, self.received = partial, landed, received
        self.send_sems, self.receive_sems = send_sems, receive_sems
        self.outs, self.jobs = outs, jobs
        row, column = lax.axis_index("rows"), lax.axis_index("cols")
        self.core = column % 2
        self.twin = (row, column + 1 - 2 * self.core)
        self.bits = [(row // (1 << bit)) % 2 for bit in range(PAIR_BITS)]
        self.partners = [
            (row + (1 - 2 * self.bits[bit]) * (1 << bit), column) for bit in range(PAIR_BITS)
        ]
        self.spans = {}
        for rows, colour in sorted({(job.rows, job.colour) for job in jobs}):
            base, size, kept, sent = 0, rows, [], []
            for bit in ORDERS[colour]:
                size //= 2
                sent.append((base + (1 - self.bits[bit]) * size, size))
                base = base + self.bits[bit] * size
                kept.append((base, size))
            self.spans[rows, colour] = (kept, sent)

    def greet(self):
        barrier = pltpu.get_barrier_semaphore()
        for partner in [self.twin] + self.partners:
            pl.semaphore_signal(
                barrier, inc=1, device_id=partner, device_id_type=pl.DeviceIdType.MESH
            )
        pl.semaphore_wait(barrier, 1 + PAIR_BITS)

    def copy(self, job, stage, source, target, partner):
        return pltpu.make_async_remote_copy(
            src_ref=source,
            dst_ref=target,
            send_sem=self.send_sems.at[job.number, stage],
            recv_sem=self.receive_sems.at[job.number, stage],
            device_id=partner,
            device_id_type=pl.DeviceIdType.MESH,
        )

    def rows_of(self, job, span):
        start, size = span
        return pl.ds(pl.multiple_of(job.lift + start, 16), size)

    def stage(self, job, stage):
        kept, sent = self.spans[job.rows, job.colour]
        order = ORDERS[job.colour]
        if stage < 4:
            source = self.partial.at[job.slot, self.rows_of(job, sent[stage])]
            start, size = job.received(stage)
            target = self.received.at[job.slot, pl.ds(start, size)]
            return self.copy(job, stage, source, target, self.partners[order[stage]])
        if stage < 8:
            source = self.landed.at[job.slot, self.rows_of(job, kept[7 - stage])]
            return self.copy(job, stage, source, source, self.partners[order[7 - stage]])
        rows = pl.ds(job.lift, job.rows)
        return self.copy(
            job, stage, self.landed.at[job.slot, rows], self.outs[job.number], self.twin
        )

    def arrival(self, job, stage):
        kept, sent = self.spans[job.rows, job.colour]
        if 4 <= stage < 8:
            target = self.landed.at[job.slot, self.rows_of(job, sent[7 - stage])]
            order = ORDERS[job.colour]
            return self.copy(job, stage, target, target, self.partners[order[7 - stage]])
        return self.stage(job, stage)

    def twin_copy(self, job, source):
        target = self.landed.at[job.slot, pl.ds(job.lift, job.rows)]
        return self.copy(job, 9, source, target, self.twin)

    def keep_copy(self, job):
        return pltpu.make_async_copy(
            self.landed.at[job.slot, pl.ds(job.lift, job.rows)],
            self.outs[job.number],
            self.send_sems.at[job.number, 10],
        )

    def run(self, number, task):
        job = self.jobs[number]
        kept, _ = self.spans[job.rows, job.colour]
        if task == 0:
            rows = pl.ds(job.lift, job.rows)
            self.twin_copy(job, self.landed.at[job.slot, rows]).wait_recv()
            self.partial[job.slot, rows, :] += self.landed[job.slot, rows, :]
        elif task <= 4:
            self.arrival(job, task - 1).wait_recv()
            start, size = job.received(task - 1)
            rows = self.rows_of(job, kept[task - 1])
            total = self.partial[job.slot, rows, :] + self.received[job.slot, pl.ds(start, size), :]
            if task < 4:
                self.partial[job.slot, rows, :] = total
            else:
                self.landed[job.slot, rows, :] = total
        elif task <= 8:
            self.arrival(job, task - 1).wait_recv()
        if task < 8:
            self.stage(job, task).start()
        elif task == 8:
            self.keep_copy(job).start()
            if job.gathered:
                self.stage(job, 8).start()
        else:
            self.arrival(job, 8).wait_recv()

    def finish(self):
        for job in self.jobs:
            for stage in range(8):
                self.stage(job, stage).wait_send()
            if job.gathered:
                self.stage(job, 8).wait_send()
            self.keep_copy(job).wait()


def gradient_kernel(
    activation,
    slope,
    in_weights,
    out_weights,
    first_low,
    grad_pre2,
    normed1,
    scale1,
    first_gain,
    output_weight,
    vectors,
    context,
    prob,
    query,
    key,
    value,
    key_table,
    query_table,
    tokens,
    pos_rows,
    query_weight,
    key_weight,
    value_weight,
    spread,
    in_share,
    out_share,
    heads_share,
    output_share,
    table_share,
    tokens_grad,
    vector_sums,
    partial,
    landed,
    received,
    leaving,
    hidden,
    narrow,
    heads_in,
    tables_in,
    weights_in,
    turned,
    grad_scores,
    flip_sums,
    key_turned_sum,
    query_turned_sum,
    value_turned_sum,
    table_sum,
    matrix,
    grad_pos_keys,
    grad_pos_queries,
    grad_total,
    normed_in,
    scale_in,
    vector_steps,
    vector_received,
    send_sems,
    receive_sems,
    vector_send_sems,
    vector_receive_sems,
    prob_sems,
    load_sems,
):
    length, width = tokens.shape
    parts, _, units = in_weights.shape
    table = pos_rows.shape[0]
    half = width // 2
    factor = 1.0 / math.sqrt(3 * HEAD_DIM)
    core = lax.axis_index("cols") % 2
    own = pl.multiple_of(core * half, half)
    jobs = make_jobs(width, table)
    outs = []
    for chunk in range(2):
        for part in range(2):
            outs.append(out_share.at[pl.ds(chunk * width, width), pl.ds(part * half, half)])
    for chunk in range(2):
        for part in range(2):
            outs.append(in_share.at[:, pl.ds(chunk * width + part * half, half)])
    outs.append(output_share.at[:, pl.ds(own, half)])
    for third in range(THIRDS):
        outs.append(heads_share.at[2 * third + core])
    for part in range(2):
        outs.append(table_share.at[pl.ds(part * table // 2, table // 2), pl.ds(own, half)])
    exchange = Exchange(partial, landed, received, send_sems, receive_sems, outs, jobs)
    mover = Mover(load_sems)

    sides = ((1 - core, 0), (core, 0), (1 - core, 1), (core, 1))

    def hidden_columns(number):
        side, chunk = sides[number]
        return pl.ds(pl.multiple_of(side * 2 * width + chunk * width, width), width)

    def load_weights(number):
        side, chunk = sides[number]
        piece = min(units, width)
        copies = []
        for start in range(0, width, piece):
            unit = chunk * width + start
            part, offset = 2 * (unit // units) + side, unit % units
            inside = pl.ds(start, piece)
            copies.append(
                mover.start(
                    out_weights.at[part, pl.ds(offset, piece)],
                    weights_in.at[2 + number % 2, inside],
                )
            )
            copies.append(
                mover.start(
                    in_weights.at[part, :, pl.ds(offset, piece)],
                    weights_in.at[number % 2, :, inside],
                )
            )
        return copies

    def load_hidden(source, number, slot):
        return mover.start(source.at[:, hidden_columns(number)], hidden.at[slot // 2, slot % 2])

    total_load = mover.start(grad_pre2, grad_total)
    active_loads = [load_hidden(activation, number, number) for number in range(4)]
    first_load = mover.start(first_low, narrow.at[0])
    weight_loads = [load_weights(number) for number in range(2)]
    vector_load = mover.start(vectors, vector_steps.at[0])
    norm_loads = (mover.start(normed1, normed_in), mover.start(scale1, scale_in))
    context_load = mover.start(context, narrow.at[2])
    head_loads = [
        mover.start(item, heads_in.at[place]) for place, item in enumerate((query, key, value))
    ]
    head_loads += [
        mover.start(key_table, tables_in.at[0]),
        mover.start(query_table, tables_in.at[1]),
    ]
    exchange.greet()

    def run_tasks(name):
        for number, task in TASKS_AFTER.get(name, ()):
            if number < JOB_COUNT:
                exchange.run(number, task)
            else:
                vector_task(task)

    vector_partners = [exchange.twin] + exchange.partners

    def vector_copy(step):
        return pltpu.make_async_remote_copy(
            src_ref=vector_steps.at[step],
            dst_ref=vector_received.at[step],
            send_sem=vector_send_sems.at[step],
            recv_sem=vector_receive_sems.at[step],
            device_id=vector_partners[step],
            device_id_type=pl.DeviceIdType.MESH,
        )

    def vector_task(step):
        if step > 0:
            vector_copy(step - 1).wait_recv()
            vector_steps[step] = vector_steps[step - 1] + vector_received[step - 1]
        if step < len(vector_partners):
            vector_copy(step).start()
        else:
            vector_sums[...] = vector_steps[step]

    def leaving_copy(number):
        job = jobs[number]
        return exchange.twin_copy(job, leaving.at[number % LEAVING, pl.ds(0, job.rows)])

    def open_space(number):
        if number >= LEAVING:
            leaving_copy(number - LEAVING).wait_send()
        return leaving.at[number % LEAVING, pl.ds(0, jobs[number].rows)]

    lower = [slice(0, half), slice(half, width)]

    def place_hidden(side, number, part_of):
        if side == 0:
            targets = [open_space(number), open_space(number + 1)]
        else:
            targets = [partial.at[number], partial.at[number + 1]]
        for rows in lower:
            value = part_of(rows).astype(LOW)
            for target, columns in zip(targets, lower):
                target[rows, :] = value[:, columns]
        if side == 0:
            leaving_copy(number).start()
            leaving_copy(number + 1).start()

    def place_halves(number, rows_list, part_of):
        job = jobs[number]
        space = open_space(number)
        for rows in rows_list:
            value = part_of(rows).astype(LOW)
            left, right = value[:, :half], value[:, half:]
            inside = pl.ds(job.lift + rows.start, rows.stop - rows.start)
            space[rows, :] = jnp.where(core == 0, right, left)
            partial[job.slot, inside, :] = jnp.where(core == 0, left, right)
        leaving_copy(number).start()

    total_load.wait()
    grad_ffn = narrow.at[1]
    grad_ffn[...] = grad_total[...].astype(LOW)
    slope_loads = []
    for number in range(4):
        side, chunk = number % 2, number // 2
        active_loads[number].wait()
        space = hidden.at[number // 2, number % 2]
        place_hidden(side, 2 * chunk, lambda rows: dot_columns(space[:, rows], grad_ffn[...]))
        slope_loads.append(load_hidden(slope, number, number))
        if side == 1:
            run_tasks(("out", chunk))

    first_load.wait()
    first_turned = turned.at[0]
    first_turned[...] = narrow[0].T
    token_loads = [mover.start(tokens, narrow.at[0])]
    for number in range(4):
        side, chunk = number % 2, number // 2
        for copy in weight_loads[number]:
            copy.wait()
        slope_loads[number].wait()
        space = hidden.at[number // 2, number % 2]
        part = dot_rows(grad_ffn[...], weights_in[2 + number % 2])
        space[...] = (part * space[...].astype(F32)).astype(LOW)
        place_hidden(side, 4 + 2 * chunk, lambda rows: dot(first_turned[rows, :], space[...]))
        grad_total[...] += dot_rows(space[...], weights_in[number % 2])
        if number + 2 < 4:
            weight_loads.append(load_weights(number + 2))
        run_tasks(("in", number))

    token_loads.append(mover.start(pos_rows, narrow.at[1]))
    output_load = mover.start(output_weight, weights_in.at[0])
    late_loads = [
        mover.start(item, weights_in.at[1 + place])
        for place, item in enumerate((query_weight, key_weight, value_weight))
    ]

    def prob_load(pair, slot):
        return pltpu.make_async_copy(
            prob.at[pl.ds(2 * pair, 2)],
            hidden.at[slot, :, :, pl.ds(0, length)],
            prob_sems.at[slot],
        )

    prob_load(0, 0).start()

    for copy in norm_loads:
        copy.wait()
    vector_load.wait()
    grad_first = grad_total[...]
    vector_steps[0, 2:3, :] = jnp.sum(grad_first * normed_in[...], axis=0, keepdims=True)
    vector_steps[0, 3:4, :] = jnp.sum(grad_first, axis=0, keepdims=True)
    grad_total[...] = norm_backward(grad_first, normed_in[...], scale_in[...], as_row(first_gain))
    narrow[3] = grad_total[...].astype(LOW)
    output_load.wait()
    heads_in[3] = dot_rows(narrow[3], weights_in[0]).astype(LOW)
    run_tasks(("norm", 0))

    context_load.wait()
    context_turned = turned.at[1]
    context_turned[...] = narrow[2].T

    place_halves(8, lower, lambda rows: dot(context_turned[rows, :], narrow[3]))
    run_tasks(("context", 0))

    for copy in head_loads:
        copy.wait()
    flip = flip_matrix()
    matrix[...] = spread_matrix(spread, table).T
    (
        query_turned,
        grad_turned,
        query_flip_turned,
        key_flip_turned,
        key_turned,
        tokens_turned,
        pos_turned,
    ) = (turned.at[place] for place in range(7))
    for copy in token_loads:
        copy.wait()
    tokens_turned[...] = narrow[0].T
    pos_turned[...] = narrow[1].T
    grads = narrow
    query_in, key_in, value_in, grad_in = (heads_in.at[place] for place in range(4))
    query_turned[...] = query_in[...].T
    key_turned[...] = key_in[...].T
    grad_turned[...] = grad_in[...].T
    blocks = [slice(at * LANES, (at + 1) * LANES) for at in range(length // LANES)]
    for rows in blocks:
        query_flip_turned[:, rows] = dot(flip, query_in[rows, :]).astype(LOW).T
        key_flip_turned[:, rows] = dot(flip, key_in[rows, :]).astype(LOW).T
    run_tasks(("prepare", 0))

    spans = [slice(side * HEAD_DIM, (side + 1) * HEAD_DIM) for side in range(2)]

    def unskew_pair(pair, straight_turned, flip_turned, table_in, scores_of, turned_sum, table_sum):
        columns = pair_columns(pair)
        head_rows = [
            pl.ds(pl.multiple_of(pair * LANES + side * HEAD_DIM, HEAD_DIM), HEAD_DIM)
            for side in range(2)
        ]
        table_sum[...] = jnp.zeros_like(table_sum)
        straight = [None, None]
        flips = []
        for rows in blocks:
            start = length - rows.stop
            window = slice(start, start + length + LANES)
            moved = []
            for side in range(2):
                left = jnp.concatenate([flip, straight_turned[head_rows[side], rows]], axis=0)
                mixed = scores_of(left, side, rows)
                part = mixed[LANES:]
                straight[side] = part if straight[side] is None else straight[side] + part
                moved.append(unskewed(mixed[:LANES]).astype(LOW))
            for side in range(2):
                table_sum[spans[side], window] += dot(
                    flip_turned[head_rows[side], rows], moved[side]
                )
            stacked = dot(jnp.concatenate(moved, axis=0), table_in[window, columns])
            flips.append(join_heads(stacked))
        for side in range(2):
            turned_sum[spans[side], :] = straight[side]
        return flips

    def pair_tasks(pair, phase):
        for place in range(width // LANES):
            name = ("head", 3 * place + phase)
            if name in TASKS_AFTER:

                @pl.when(pair == place)
                def _():
                    run_tasks(name)

    def send_third(third):
        number = TABLE_JOBS - THIRDS + third
        wide = 2 * LANES
        columns = pl.ds(pl.multiple_of(third * wide, wide), wide)
        job = Job(number, width, 0, number, 0, True)
        before = Job(number - LEAVING, width, 0, number - LEAVING, 0, True)
        space = leaving.at[lax.rem(number, LEAVING)]
        exchange.twin_copy(before, space).wait_send()
        query_grad = dot(tokens_turned[...], grads[0, :, columns])
        query_grad = query_grad + dot_rows(pos_turned[...], grad_pos_queries[columns, :])
        key_grad = dot(tokens_turned[...], grads[1, :, columns])
        key_grad = key_grad + dot_rows(pos_turned[...], grad_pos_keys[columns, :])
        value_grad = dot(tokens_turned[...], grads[2, :, columns])
        for place, value in enumerate((query_grad * factor, key_grad, value_grad)):
            lanes = slice(place * LANES, (place + 1) * LANES)
            low, high = value[:, :LANES].astype(LOW), value[:, LANES:].astype(LOW)
            space[:, lanes] = jnp.where(core == 0, high, low)
            partial[number, :, lanes] = jnp.where(core == 0, low, high)
        exchange.twin_copy(job, space).start()

    def pair_back(pair, carry):
        slot = lax.rem(pair, 2)
        columns = pair_columns(pair)
        pair_rows = pl.ds(pl.multiple_of(pair * LANES, LANES), LANES)
        prob_load(pair, slot).wait()

        @pl.when(pair + 1 < width // LANES)
        def _():
            prob_load(pair + 1, 1 - slot).start()

        value_pair = value_in[:, columns].T
        for rows in blocks:
            grad_probs = dot(both_heads(grad_in[rows, columns]), value_pair)
            for side in range(2):
                weights = hidden[slot, side, rows, 0:length].astype(F32)
                product = grad_probs[side * LANES : (side + 1) * LANES] * weights
                shared = jnp.sum(product, axis=-1, keepdims=True)
                grad_scores[side, rows, :] = (product - weights * shared).astype(LOW)
        for side in range(2):
            head_rows = pl.ds(
                pl.multiple_of(pair * LANES + side * HEAD_DIM, HEAD_DIM), HEAD_DIM
            )
            value_turned_sum[spans[side], :] = dot(
                grad_turned[head_rows, :], hidden[slot, side, :, 0:length]
            )
        grads[2, :, columns] = value_turned_sum[...].astype(LOW).T
        pair_tasks(pair, 0)
        flips = unskew_pair(
            pair,
            query_turned,
            query_flip_turned,
            tables_in.at[0],
            lambda left, side, rows: dot(left, grad_scores[side, rows, :]),
            key_turned_sum,
            table_sum,
        )
        for rows, part in zip(blocks, flips):
            flip_sums[rows, :] = split_flip(flip, part)
        summed = dot(table_sum[...].astype(LOW), matrix[...])
        grad_pos_keys[pair_rows, :] = summed.astype(LOW)
        pair_tasks(pair, 1)
        flips = unskew_pair(
            pair,
            key_turned,
            key_flip_turned,
            tables_in.at[1],
            lambda left, side, rows: dot_rows(left, grad_scores[side, :, rows]),
            query_turned_sum,
            table_sum,
        )
        for rows, part in zip(blocks, flips):
            summed = key_turned_sum[:, rows].T + split_flip(flip, part)
            grads[1, rows, columns] = summed.astype(LOW)
            summed = query_turned_sum[:, rows].T + flip_sums[rows, :]
            grads[0, rows, columns] = summed.astype(LOW)
        summed = dot(table_sum[...].astype(LOW), matrix[...])
        grad_pos_queries[pair_rows, :] = summed.astype(LOW)

        @pl.when(lax.rem(pair, 2) == 1)
        def _():
            send_third(pair // 2)

        pair_tasks(pair, 2)
        return carry

    lax.fori_loop(0, width // LANES, pair_back, 0)

    for copy in late_loads:
        copy.wait()

    for part in range(2):
        shift = part * table // 2
        rows = slice(0, table // 2)

        def table_part(rows):
            inside = slice(shift + rows.start, shift + rows.stop)
            turned_dims = (((0,), (1,)), ((), ()))
            summed = lax.dot_general(
                grad_pos_keys[:, inside], weights_in[2], turned_dims, preferred_element_type=F32
            )
            return summed + factor * lax.dot_general(
                grad_pos_queries[:, inside], weights_in[1], turned_dims, preferred_element_type=F32
            )

        place_halves(TABLE_JOBS + part, [rows], table_part)
    run_tasks(("table", 0))
    tokens_grad_low = narrow.at[3]
    for rows in blocks:
        summed = grad_total[rows, :] + factor * dot_rows(grads[0, rows, :], weights_in[1])
        summed = summed + dot_rows(grads[1, rows, :], weights_in[2])
        summed = summed + dot_rows(grads[2, rows, :], weights_in[3])
        tokens_grad_low[rows, :] = summed.astype(LOW)
    mover.leave(tokens_grad_low, tokens_grad)
    run_tasks(("tail", 0))
    exchange.finish()
    for number in range(JOB_COUNT - LEAVING, JOB_COUNT):
        leaving_copy(number).wait_send()
    for step in range(len(vector_partners)):
        vector_copy(step).wait_send()
    mover.finish()


def gradients(
    activation,
    slope,
    in_weights,
    out_weights,
    first_low,
    grad_pre2,
    normed1,
    scale1,
    first_gain,
    output_weight,
    vectors,
    context,
    prob,
    query,
    key,
    value,
    key_table,
    query_table,
    tokens,
    pos_rows,
    query_weight,
    key_weight,
    value_weight,
):
    length, width = tokens.shape
    table = pos_rows.shape[0]
    half = width // 2
    inputs = (
        activation,
        slope,
        in_weights,
        out_weights,
        first_low,
        grad_pre2,
        normed1,
        scale1,
        first_gain,
        output_weight,
        vectors,
        context,
        prob,
        query,
        key,
        value,
        key_table,
        query_table,
        tokens,
        pos_rows,
        query_weight,
        key_weight,
        value_weight,
        jnp.asarray(spread_index(length)),
    )
    anywhere = pl.BlockSpec(memory_space=pl.ANY)
    local = pl.BlockSpec(memory_space=pltpu.VMEM)
    outs = [
        jax.ShapeDtypeStruct((width, 2 * width), LOW),
        jax.ShapeDtypeStruct((2 * width, width), LOW),
        jax.ShapeDtypeStruct((2 * THIRDS, width, half), LOW),
        jax.ShapeDtypeStruct((width, width), LOW),
        jax.ShapeDtypeStruct((table, width), LOW),
        jax.ShapeDtypeStruct((length, width), LOW),
        jax.ShapeDtypeStruct(vectors.shape, F32),
    ]
    slots = TABLE_JOBS + 1
    scratch = [
        pltpu.VMEM((slots, width, half), LOW),
        pltpu.VMEM((slots, width, half), LOW),
        pltpu.VMEM((slots, width // 16 * 15, half), LOW),
        pltpu.VMEM((LEAVING, width, half), LOW),
        pltpu.VMEM((2, 2, length, width), LOW),
        pltpu.VMEM((4, length, width), LOW),
        pltpu.VMEM((4, length, width), LOW),
        pltpu.VMEM((2, 2 * length, width), LOW),
        pltpu.VMEM((4, width, width), LOW),
        pltpu.VMEM((7, width, length), LOW),
        pltpu.VMEM((2, length, length), LOW),
        pltpu.VMEM((length, LANES), F32),
        pltpu.VMEM((LANES, length), F32),
        pltpu.VMEM((LANES, length), F32),
        pltpu.VMEM((LANES, length), F32),
        pltpu.VMEM((LANES, 2 * length), F32),
        pltpu.VMEM((2 * length, table), LOW),
        pltpu.VMEM((width, table), LOW),
        pltpu.VMEM((width, table), LOW),
        pltpu.VMEM((length, width), F32),
        pltpu.VMEM((length, width), F32),
        pltpu.VMEM((length, 1), F32),
        pltpu.VMEM((2 + PAIR_BITS,) + vectors.shape, F32),
        pltpu.VMEM((1 + PAIR_BITS,) + vectors.shape, F32),
        pltpu.SemaphoreType.DMA((JOB_COUNT, 11)),
        pltpu.SemaphoreType.DMA((JOB_COUNT, 10)),
        pltpu.SemaphoreType.DMA((1 + PAIR_BITS,)),
        pltpu.SemaphoreType.DMA((1 + PAIR_BITS,)),
        pltpu.SemaphoreType.DMA((2,)),
        pltpu.SemaphoreType.DMA((64,)),
    ]
    return pl.pallas_call(
        gradient_kernel,
        in_specs=[local if at in (8, 23) else anywhere for at in range(len(inputs))],
        out_specs=[anywhere] * (len(outs) - 1) + [local],
        out_shape=outs,
        scratch_shapes=scratch,
        compiler_params=pltpu.CompilerParams(
            vmem_limit_bytes=GRADIENT_VMEM_BYTES, collective_id=0, has_side_effects=True
        ),
        name="gradients",
    )(*inputs)


def finish_kernel(
    in_share,
    out_share,
    output_share,
    heads_share,
    table_share,
    position_table,
    output_in,
    tokens_in,
    vectors,
    table_gain,
    in_grad,
    out_grad,
    output_grad,
    query_grad,
    key_grad,
    value_grad,
    table_grad,
    output,
    tokens_grad,
    gain_grad,
    shift_grad,
    *rest,
):
    vector_grads, rest = rest[:4], rest[4:]
    in_low, in_wide, out_low, out_wide, output_low, output_wide, heads_low, *rest = rest
    query_wide, key_wide, value_wide, table_low, table_wide, position_in, *rest = rest
    output_space, tokens_space, sems = rest
    mover = Mover(sems)
    width = output_share.shape[0]
    half = width // 2

    def cuts(source, low, wide, target):
        pieces = []
        height = min(width, source.shape[0])
        for start in range(0, source.shape[0], height):
            rows = pl.ds(start, height)
            pieces.append(
                (mover.start(source.at[rows], low.at[rows]), low, wide, target, rows)
            )
        return pieces

    pieces = cuts(in_share, in_low, in_wide, in_grad)
    pieces += cuts(out_share, out_low, out_wide, out_grad)
    pieces += cuts(output_share, output_low, output_wide, output_grad)
    head_loads = [
        mover.start(heads_share.at[:, pl.ds(start, half)], heads_low.at[:, pl.ds(start, half)])
        for start in range(0, width, half)
    ]
    table_load = mover.start(table_share, table_low)
    position_load = mover.start(position_table, position_in)
    passing = [
        (mover.start(source, space), space, target)
        for source, space, target in (
            (output_in, output_space, output),
            (tokens_in, tokens_space, tokens_grad),
        )
    ]
    for load, low, wide, target, rows in pieces:
        load.wait()
        wide[rows, :] = low[rows, :].astype(F32)
        mover.leave(wide.at[rows], target.at[rows])
    for number, load in enumerate(head_loads):
        load.wait()
        rows = slice(number * half, (number + 1) * half)
        for place, (wide, target) in enumerate(
            ((query_wide, query_grad), (key_wide, key_grad), (value_wide, value_grad))
        ):
            for block in range(2 * THIRDS):
                lanes = slice(place * LANES, (place + 1) * LANES)
                columns = slice(block * LANES, (block + 1) * LANES)
                wide[rows, columns] = heads_low[block, rows, lanes].astype(F32)
            mover.leave(wide.at[rows], target.at[rows])
    for load, space, target in passing:
        load.wait()
        mover.leave(space, target)
    table_load.wait()
    position_load.wait()
    gain = as_row(table_gain)
    grad = table_low[...].astype(F32)
    _, normed, scale_rows = norm_forward(position_in[...].astype(F32), gain, 0.0)
    table_wide[...] = norm_backward(grad, normed, scale_rows, gain)
    mover.leave(table_wide, table_grad)
    gain_grad[...] = jnp.sum(grad * normed, axis=0)
    shift_grad[...] = jnp.sum(grad, axis=0)
    for place, target in enumerate(vector_grads):
        target[...] = vectors[place, :]
    mover.finish()


def finish(shares, vectors, position_table, table_gain, output, tokens_grad):
    in_share, out_share, heads_share, output_share, table_share = shares
    table, width = position_table.shape
    inputs = (
        in_share,
        out_share,
        output_share,
        heads_share,
        table_share,
        position_table,
        output,
        tokens_grad,
        vectors,
        table_gain,
    )
    anywhere = pl.BlockSpec(memory_space=pl.ANY)
    local = pl.BlockSpec(memory_space=pltpu.VMEM)

    def wide(item):
        return jax.ShapeDtypeStruct(item.shape, F32)

    square = jax.ShapeDtypeStruct((width, width), F32)
    vector = jax.ShapeDtypeStruct((width,), F32)
    outs = [wide(in_share), wide(out_share), square, square, square, square, wide(table_share)]
    outs += [jax.ShapeDtypeStruct(item.shape, LOW) for item in (output, tokens_grad)]
    outs += [vector] * 6
    scratch = []
    for item in (in_share, out_share, output_share):
        scratch += [pltpu.VMEM(item.shape, LOW), pltpu.VMEM(item.shape, F32)]
    scratch += [pltpu.VMEM(heads_share.shape, LOW)] + [pltpu.VMEM((width, width), F32)] * 3
    scratch += [pltpu.VMEM((table, width), LOW), pltpu.VMEM((table, width), F32)]
    scratch += [pltpu.VMEM(item.shape, LOW) for item in (position_table, output, tokens_grad)]
    scratch.append(pltpu.SemaphoreType.DMA((64,)))
    return pl.pallas_call(
        finish_kernel,
        in_specs=[anywhere] * 8 + [local] * 2,
        out_specs=[anywhere] * 9 + [local] * 6,
        out_shape=outs,
        scratch_shapes=scratch,
        compiler_params=pltpu.CompilerParams(vmem_limit_bytes=VMEM_BYTES),
        name="finish",
    )(*inputs)


def beyond(shares):
    in_share, out_share, *others = shares
    chips = 1 << PAIR_BITS
    rows, columns = lax.axis_size("rows"), lax.axis_size("cols")
    if rows > chips:
        groups = [[at + chips * step for step in range(rows // chips)] for at in range(chips)]
        in_share, out_share, *others = lax.psum(
            (in_share, out_share, *others), "rows", axis_index_groups=groups
        )
    if columns > 2:
        groups = [[at + 2 * step for step in range(columns // 2)] for at in range(2)]
        others = lax.psum(tuple(others), "cols", axis_index_groups=groups)
        in_share = lax.psum_scatter(
            in_share, "cols", scatter_dimension=1, axis_index_groups=groups, tiled=True
        )
        out_share = lax.psum_scatter(
            out_share, "cols", scatter_dimension=0, axis_index_groups=groups, tiled=True
        )
    return (in_share, out_share, *others)


def on_device(
    tokens,
    segment_ids,
    position_table,
    table_gain,
    table_shift,
    query_weight,
    key_weight,
    value_weight,
    output_weight,
    first_gain,
    first_shift,
    feedforward_input_weight,
    ffn_out,
    second_gain,
    second_shift,
    out_grad,
):
    (
        query,
        key,
        value,
        prob,
        context,
        normed1,
        scale1,
        first_low,
        key_table,
        query_table,
        pos_rows,
        in_weights,
        out_weights,
        activation,
        slope,
        grad_pre2,
        output,
        vectors,
    ) = forward(
        tokens,
        segment_ids,
        position_table,
        table_gain,
        table_shift,
        query_weight,
        key_weight,
        value_weight,
        output_weight,
        first_gain,
        first_shift,
        feedforward_input_weight,
        ffn_out,
        second_gain,
        second_shift,
        out_grad,
    )
    shares = gradients(
        activation,
        slope,
        in_weights,
        out_weights,
        first_low,
        grad_pre2,
        normed1,
        scale1,
        first_gain,
        output_weight,
        vectors,
        context,
        prob,
        query,
        key,
        value,
        key_table,
        query_table,
        tokens,
        pos_rows,
        query_weight,
        key_weight,
        value_weight,
    )
    *sums, vectors = beyond(shares[:5] + shares[6:])
    (
        in_grad,
        out_weight_grad,
        output_weight_grad,
        query_grad,
        key_grad,
        value_grad,
        table_grad,
        output,
        tokens_grad,
        table_gain_grad,
        table_shift_grad,
        second_gain_grad,
        second_shift_grad,
        first_gain_grad,
        first_shift_grad,
    ) = finish(sums, vectors, position_table, table_gain, output, shares[5])
    return (
        output,
        tokens_grad,
        table_grad,
        table_gain_grad,
        table_shift_grad,
        query_grad,
        key_grad,
        value_grad,
        output_weight_grad,
        first_gain_grad,
        first_shift_grad,
        in_grad,
        out_weight_grad,
        second_gain_grad,
        second_shift_grad,
    )


def solution(mesh):
    spread = P(("rows", "cols"), None)
    in_specs = (spread, spread) + (P(),) * 9 + (P(None, "cols"), P("cols", None), P(), P(), spread)
    out_specs = (
        (spread, spread) + (P(),) * 9 + (P(None, "cols"), P("cols", None), P(), P())
    )
    return jax.shard_map(
        on_device, mesh=mesh, in_specs=in_specs, out_specs=out_specs, check_vma=False
    )
```
